256 devices in a mesh: mem: 8 (over z_lo, x), dp: 32 (over z_hi, y, core).
Axes of the slice: x: 4, y: 4, z: 8 (z_hi: 4, z_lo: 2; z = z_hi * 2 + z_lo), core: 2. Of those that a mesh axis runs over, the one named last changes fastest.
Arguments:
- member_fields: bfloat16 [32, 16, 256, 1024], P('dp', 'mem'), may hold values from -6 to 6
- weight_first: bfloat16 [7, 256, 256], P(None, 'dp'), may hold values from -0.125 to 0.125
- weight_second: bfloat16 [7, 256, 256], P(None, 'dp'), may hold values from -0.125 to 0.125
- weight_head: bfloat16 [69, 256], P(None, 'dp'), may hold values from -0.375 to 0.375
- neighbours_fine: int32 [7, 1024], replicated, may hold values from -1 to 1023, as said below
- neighbours_mid: int32 [7, 256], replicated, may hold values from -1 to 255, as said below
- parents_fine: int32 [1024], replicated, may hold values from 0 to 255, as said below
- parents_mid: int32 [256], replicated, may hold values from 0 to 63, as said below
- observations: float32 [32, 69, 64], P('dp'), may hold values from -4 to 4
Outputs:
- grad_first: float32 [7, 256, 256], P(None, 'dp')
- grad_second: float32 [7, 256, 256], P(None, 'dp')
- grad_head: float32 [69, 256], P(None, 'dp')
The draws below stay inside these ranges and needn't reach their ends.
Inputs may be any that keep to these rules, and one draw needn't show every extreme that they name: `neighbours_fine`: row 0 lists each cell itself; rows 1 to 6 list its hex neighbours among the 1024 cells of the window, -1 where a neighbour lies outside the window or is missing at a pentagon. `neighbours_mid`: row 0 lists each cell itself; rows 1 to 6 list its hex neighbours among the 256 cells of the window, -1 where a neighbour lies outside the window or is missing at a pentagon. `parents_fine`: every one of the 256 cells is the parent of exactly 4 cells. `parents_mid`: every one of the 64 cells is the parent of exactly 4 cells.
All inputs are finite; a program needn't handle non-finite values.
Results may differ from the reference program's by a relative error of at most 0.014.
Values may be sent and summed in bfloat16 or wider, within the bound.
No kernel may reach another device: no remote copies, remote signals or barrier semaphores. Data moves between devices by JAX's collectives and lax.ppermute only.
A program may use at most 64 MiB of HBM per device.

```python
import math
import jax
import jax.numpy as jnp
from jax import lax

MEMBERS = 16
CHANNELS = 256
FIELDS = 69
SLOTS = 7
CELLS_OUT = 64
CELLS_MID = 256
CELLS_IN = 1024
SAMPLES = 32


def level_ordering(key, depth_level, cell_count):
    return jax.random.permutation(jax.random.fold_in(key, 100 + depth_level), cell_count).astype(jnp.int32)


def inverse_ordering(ordering):
    cell_count = ordering.shape[0]
    return jnp.zeros((cell_count,), jnp.int32).at[ordering].set(jnp.arange(cell_count, dtype=jnp.int32))


def hex_table(key, depth_level, grid_rows, grid_cols):
    ordering = level_ordering(key, depth_level, grid_rows * grid_cols)
    inverse = inverse_ordering(ordering)
    grid_row = ordering // grid_cols
    grid_col = ordering % grid_cols
    entries = []
    for row_step, col_step in [(0, 0), (0, 1), (0, -1), (1, 0), (-1, 0), (1, -1), (-1, 1)]:
        moved_row = grid_row + row_step
        moved_col = grid_col + col_step
        inside = (moved_row >= 0) & (moved_row < grid_rows) & (moved_col >= 0) & (moved_col < grid_cols)
        landing = jnp.clip(moved_row, 0, grid_rows - 1) * grid_cols + jnp.clip(moved_col, 0, grid_cols - 1)
        entries.append(jnp.where(inside, inverse[landing], -1))
    return jnp.stack(entries).astype(jnp.int32)


def mark_pentagons(key, neighbour_table):
    cell_count = neighbour_table.shape[1]
    pentagon_cells = jax.random.randint(key, (2,), 0, cell_count)
    is_pentagon = jnp.any(jnp.arange(cell_count)[None, :] == pentagon_cells[:, None], axis=0)
    return neighbour_table.at[6].set(jnp.where(is_pentagon, -1, neighbour_table[6])).astype(jnp.int32)


def parent_table(key, depth_level, grid_rows, grid_cols):
    ordering = level_ordering(key, depth_level, grid_rows * grid_cols)
    coarse_inverse = inverse_ordering(level_ordering(key, depth_level + 1, grid_rows * grid_cols // 4))
    grid_row = ordering // grid_cols
    grid_col = ordering % grid_cols
    return coarse_inverse[grid_row // 2 * (grid_cols // 2) + grid_col // 2].astype(jnp.int32)


def draw_neighbours_fine(key, part):
    neighbour_table = hex_table(key, 0, 16, CELLS_OUT)
    key = jax.random.fold_in(key, 1)
    return mark_pentagons(key, neighbour_table)


def draw_neighbours_mid(key, part):
    neighbour_table = hex_table(key, 1, 8, CELLS_OUT // 2)
    key = jax.random.fold_in(key, 2)
    return mark_pentagons(key, neighbour_table)


def draw_parents_fine(key, part):
    return parent_table(key, 0, 16, CELLS_OUT)


def draw_parents_mid(key, part):
    return parent_table(key, 1, 8, CELLS_OUT // 2)


def block_levels(own_key, dims, split, low, largest):
    loudness, own = 1.0, jax.random.fold_in(own_key, 6)
    for position, parts in split:
        draws = jnp.exp(jax.random.uniform(jax.random.fold_in(own, position), (parts,), jnp.float32, low / len(split), largest / len(split)))
        loudness = loudness * jnp.repeat(draws, dims[position] // parts).reshape([-1 if axis == position else 1 for axis in range(len(dims))])
    return loudness


def noise(own_key, extent, deviation, limit, split=(), kind=jnp.bfloat16):
    drawn = jax.random.normal(own_key, extent, jnp.float32) * deviation
    if len(split) > 0:
        drawn = block_levels(own_key, extent, split, -0.22, 0.18) * drawn
    return jnp.clip(drawn, min=-limit, max=limit).astype(kind)


def setup_inputs(seed: int = 0) -> dict:
    splits = jax.random.split(jax.random.key(seed), 10)
    return {
        "member_fields": noise(splits[0], (SAMPLES, MEMBERS, CHANNELS, CELLS_IN), 1.0, 6.0, ((0, 32), (1, 8))),
        "weight_first": noise(splits[1], (SLOTS, CHANNELS, CHANNELS), (SLOTS * CHANNELS) ** -0.5, 0.125, ((1, 32),)),
        "weight_second": noise(splits[2], (SLOTS, CHANNELS, CHANNELS), (SLOTS * CHANNELS) ** -0.5, 0.125, ((1, 32),)),
        "weight_head": noise(splits[3], (FIELDS, CHANNELS), CHANNELS ** -0.5, 0.375, ((1, 32),)),
        "neighbours_fine": draw_neighbours_fine(jax.random.fold_in(splits[9], 71), 0),
        "neighbours_mid": draw_neighbours_mid(jax.random.fold_in(splits[9], 71), 0),
        "parents_fine": draw_parents_fine(jax.random.fold_in(splits[9], 71), 0),
        "parents_mid": draw_parents_mid(jax.random.fold_in(splits[9], 71), 0),
        "observations": noise(splits[8], (SAMPLES, FIELDS, CELLS_OUT), 0.5, 4.0, ((0, 32),), jnp.float32),
    }


SMOOTH = 0.0001

def silu_slope(preact):
    sigmoid_value = jax.nn.sigmoid(preact)
    return sigmoid_value * (1.0 + preact * (1.0 - sigmoid_value))

def slot_tiles(fields, neighbours):
    present = (neighbours >= 0).astype(fields.dtype)
    gathered = jnp.take(fields, jnp.maximum(neighbours, 0).reshape(-1), axis=2)
    gathered = gathered.reshape(fields.shape[0], fields.shape[1], neighbours.shape[0], neighbours.shape[1])
    return gathered * present

def pool_cells(fields, parents, coarse):
    moved = jnp.moveaxis(fields.astype(jnp.float32), 2, 0)
    summed = jax.ops.segment_sum(moved, parents, num_segments=coarse)
    return jnp.moveaxis(summed, 0, 2) * 0.25

def score_derivative(local_members, member_cohort, truth_states, normalizing_multiplier):
    ensemble_size = member_cohort.shape[0]
    error_term = local_members - truth_states[None]
    skill_term = error_term / jnp.sqrt(error_term * error_term + SMOOTH) / ensemble_size
    pairwise = local_members[:, None] - member_cohort[None, :]
    spread_term = lax.optimization_barrier(jnp.sum(pairwise / jnp.sqrt(pairwise * pairwise + SMOOTH), axis=1)) / (ensemble_size * (ensemble_size - 1))
    return normalizing_multiplier * (skill_term - spread_term)

def reference(member_fields, weight_first, weight_second, weight_head, neighbours_fine, neighbours_mid, parents_fine, parents_mid, observations):
    first_wide = weight_first.astype(jnp.float32)
    second_wide = weight_second.astype(jnp.float32)
    readout_replicated = weight_head.astype(jnp.float32)
    normalizing_multiplier = MEMBERS / math.sqrt(SAMPLES * CELLS_OUT)
    mid_present = (neighbours_mid >= 0).astype(jnp.float32)
    mid_index = jnp.maximum(neighbours_mid, 0).reshape(-1)

    def one_sample(carry, inputs):
        fields_in, truth_states = inputs
        tiles_in = slot_tiles(fields_in, neighbours_fine).astype(jnp.float32)
        pre_first = jnp.einsum('joi,mijn->mon', first_wide, tiles_in)
        hidden_first = (fields_in.astype(jnp.float32) + jax.nn.silu(pre_first)).astype(jnp.bfloat16)
        fields_mid = pool_cells(hidden_first, parents_fine, CELLS_MID).astype(jnp.bfloat16)
        tiles_mid = slot_tiles(fields_mid, neighbours_mid).astype(jnp.float32)
        pre_second = jnp.einsum('joi,mijn->mon', second_wide, tiles_mid)
        hidden_second = (fields_mid.astype(jnp.float32) + jax.nn.silu(pre_second)).astype(jnp.bfloat16)
        output_fields = pool_cells(hidden_second, parents_mid, CELLS_OUT).astype(jnp.bfloat16)
        result_replicated = output_fields.astype(jnp.float32)
        predicted_states = jnp.einsum('mt,ctq->cmq', readout_replicated, result_replicated)
        predicted_derivative = score_derivative(predicted_states, predicted_states, truth_states, normalizing_multiplier).astype(jnp.bfloat16)
        slope_wide = predicted_derivative.astype(jnp.float32)
        grad_head = jnp.einsum('mfp,mcp->fc', slope_wide, result_replicated)
        back_out = jnp.einsum('fc,mfp->mcp', readout_replicated, slope_wide)
        back_second = jnp.take(back_out, parents_mid, axis=2) * 0.25
        slope_second = (back_second * silu_slope(pre_second)).astype(jnp.bfloat16).astype(jnp.float32)
        grad_second = jnp.einsum('mon,mijn->joi', slope_second, tiles_mid)
        spread_back = jnp.einsum('joi,mon->mijn', second_wide, slope_second) * mid_present
        spread_back = spread_back.reshape(spread_back.shape[0], spread_back.shape[1], -1)
        back_mid = back_second.at[:, :, mid_index].add(spread_back)
        back_first = jnp.take(back_mid, parents_fine, axis=2) * 0.25
        slope_first = (back_first * silu_slope(pre_first)).astype(jnp.bfloat16).astype(jnp.float32)
        grad_first = jnp.einsum('mon,mijn->joi', slope_first, tiles_in)
        return ((carry[0] + grad_first, carry[1] + grad_second, carry[2] + grad_head), None)
    start = (jnp.zeros((SLOTS, CHANNELS, CHANNELS), jnp.float32), jnp.zeros((SLOTS, CHANNELS, CHANNELS), jnp.float32), jnp.zeros((FIELDS, CHANNELS), jnp.float32))
    totals, unused = lax.scan(one_sample, start, (member_fields, observations))
    return (totals[0], totals[1], totals[2])
```

```python
import math

import jax
import jax.numpy as jnp
from jax import lax
from jax.experimental import pallas as pl
from jax.experimental.pallas import tpu as pltpu
from jax.sharding import Mesh
from jax.sharding import PartitionSpec as P

DP = ("z_hi", "y", "core")
MEM = ("z_lo", "x")

MEMBERS = 16
CHANNELS = 256
SLOTS = 7
FIELDS = 69
FIELD_ROWS = 72
CELLS_OUT = 64
CELLS_MID = 256
CELLS_IN = 1024
SAMPLES = 32
LOCAL = 2
PIECE = 512
SMOOTH = 0.0001
NORM = MEMBERS / math.sqrt(SAMPLES * CELLS_OUT)
SECOND_AT = SLOTS * CHANNELS
HEAD_AT = 2 * SLOTS * CHANNELS
WIDTH = 4096
VMEM_BYTES = 48 * 1024 * 1024

f32 = jnp.float32
bf16 = jnp.bfloat16


def dot(a, b):
    return lax.dot_general(a, b, (((1,), (0,)), ((), ())), preferred_element_type=f32)


def dot_bt(a, b):
    return lax.dot_general(a, b, (((1,), (1,)), ((), ())), preferred_element_type=f32)


def dot_at(a, b):
    return lax.dot_general(a, b, (((0,), (0,)), ((), ())), preferred_element_type=f32)


def one_hot(index_row, rows):
    shape = (rows, index_row.shape[1])
    return jnp.where(lax.broadcasted_iota(jnp.int32, shape, 0) == index_row, 1.0, 0.0).astype(bf16)


def tiles_kernel(x_ref, nb_ref, out_ref):
    tile = dot(x_ref[...], one_hot(nb_ref[0], CELLS_IN)).astype(bf16)
    for m in range(LOCAL):
        out_ref[m, 0] = tile[m * CHANNELS : (m + 1) * CHANNELS]


def fine_tiles(x0, nb):
    return pl.pallas_call(
        tiles_kernel,
        grid=(SLOTS - 1,),
        in_specs=[
            pl.BlockSpec((LOCAL * CHANNELS, CELLS_IN), lambda j: (0, 0)),
            pl.BlockSpec((1, 1, CELLS_IN), lambda j: (j, 0, 0)),
        ],
        out_specs=pl.BlockSpec((LOCAL, 1, CHANNELS, CELLS_IN), lambda j: (0, j, 0, 0)),
        out_shape=jax.ShapeDtypeStruct((LOCAL, SLOTS - 1, CHANNELS, CELLS_IN), bf16),
        compiler_params=pltpu.CompilerParams(vmem_limit_bytes=VMEM_BYTES),
        cost_estimate=pl.CostEstimate(flops=6_500_000_000, bytes_accessed=8_000_000, transcendentals=0),
        name="fine_tiles",
    )(x0, nb)


def forward_kernel(
    place_ref, mine_ref, other_ref, x_ref, tiles_ref, parents_ref, nb_mid_ref, parents_mid_ref,
    slope1_ref, w_ref, tiles_mid_ref, slope2_ref, x2_ref, pred_ref, pooled_ref,
):
    m, k = pl.program_id(0), pl.program_id(1)

    @pl.when((m == 0) & (k == 0))
    def _():
        core, z = place_ref[0], place_ref[1]
        for source, here in ((mine_ref, core), (other_ref, 1 - core)):
            for x in range(4):
                column = pl.multiple_of(x * 2 * PIECE + here * PIECE, PIECE)
                for y in range(4):
                    for back in range(4):
                        row = pl.multiple_of((lax.rem(z - back + 4, 4) * 4 + y) * 16, 16)
                        w_ref[pl.ds(row, 16), pl.ds(column, PIECE)] = source[x * 4 + y, back]

    a1 = dot(w_ref[:, 0:CHANNELS], x_ref[0])
    for j in range(1, SLOTS):
        a1 = a1 + dot(w_ref[:, j * CHANNELS : (j + 1) * CHANNELS], tiles_ref[0, j - 1])
    gate = jax.nn.sigmoid(a1)
    slope1_ref[0] = (gate * (1.0 + a1 * (1.0 - gate))).astype(bf16)
    h1 = (x_ref[0].astype(f32) + a1 * gate).astype(bf16)
    part = dot_bt(h1, one_hot(parents_ref[...], CELLS_MID))

    @pl.when(k == 0)
    def _():
        pooled_ref[m] = part

    @pl.when(k > 0)
    def _():
        pooled_ref[m] += part

    @pl.when((m == LOCAL - 1) & (k == pl.num_programs(1) - 1))
    def _():
        x1 = (pooled_ref[...].reshape(LOCAL * CHANNELS, CELLS_MID) * 0.25).astype(bf16)
        for i in range(LOCAL):
            tiles_mid_ref[i, 0:CHANNELS] = x1[i * CHANNELS : (i + 1) * CHANNELS]
        for j in range(1, SLOTS):
            tile = dot(x1, one_hot(nb_mid_ref[j : j + 1, :], CELLS_MID)).astype(bf16)
            for i in range(LOCAL):
                tiles_mid_ref[i, j * CHANNELS : (j + 1) * CHANNELS] = tile[i * CHANNELS : (i + 1) * CHANNELS]
        pool = one_hot(parents_mid_ref[...], CELLS_OUT)
        for i in range(LOCAL):
            a2 = dot(w_ref[:, SECOND_AT:HEAD_AT], tiles_mid_ref[i])
            gate2 = jax.nn.sigmoid(a2)
            slope2_ref[i] = gate2 * (1.0 + a2 * (1.0 - gate2))
            h2 = (x1[i * CHANNELS : (i + 1) * CHANNELS].astype(f32) + a2 * gate2).astype(bf16)
            x2_ref[:, i * CELLS_OUT : (i + 1) * CELLS_OUT] = (dot_bt(h2, pool) * 0.25).astype(bf16)
        pred = dot_at(w_ref[:, HEAD_AT : HEAD_AT + 128], x2_ref[...])
        pred_ref[...] = pred[0:FIELD_ROWS]


def forward(place, mine, other, x0, tiles, parents_fine, nb_mid, parents_mid):
    chunk = 256
    whole = lambda *shape: pl.BlockSpec(shape, lambda m, k: (0,) * len(shape))
    return pl.pallas_call(
        forward_kernel,
        grid=(LOCAL, CELLS_IN // chunk),
        in_specs=[
            pl.BlockSpec(memory_space=pltpu.SMEM),
            whole(16, 4, 16, PIECE),
            whole(16, 4, 16, PIECE),
            pl.BlockSpec((1, CHANNELS, chunk), lambda m, k: (m, 0, k)),
            pl.BlockSpec((1, SLOTS - 1, CHANNELS, chunk), lambda m, k: (m, 0, 0, k)),
            pl.BlockSpec((1, chunk), lambda m, k: (0, k)),
            whole(SLOTS, CELLS_MID),
            whole(1, CELLS_MID),
        ],
        out_specs=[
            pl.BlockSpec((1, CHANNELS, chunk), lambda m, k: (m, 0, k)),
            whole(CHANNELS, WIDTH),
            whole(LOCAL, SECOND_AT, CELLS_MID),
            whole(LOCAL, CHANNELS, CELLS_MID),
            whole(CHANNELS, LOCAL * CELLS_OUT),
            whole(FIELD_ROWS, LOCAL * CELLS_OUT),
        ],
        out_shape=[
            jax.ShapeDtypeStruct((LOCAL, CHANNELS, CELLS_IN), bf16),
            jax.ShapeDtypeStruct((CHANNELS, WIDTH), bf16),
            jax.ShapeDtypeStruct((LOCAL, SECOND_AT, CELLS_MID), bf16),
            jax.ShapeDtypeStruct((LOCAL, CHANNELS, CELLS_MID), f32),
            jax.ShapeDtypeStruct((CHANNELS, LOCAL * CELLS_OUT), bf16),
            jax.ShapeDtypeStruct((FIELD_ROWS, LOCAL * CELLS_OUT), f32),
        ],
        scratch_shapes=[pltpu.VMEM((LOCAL, CHANNELS, CELLS_MID), f32)],
        compiler_params=pltpu.CompilerParams(vmem_limit_bytes=VMEM_BYTES),
        cost_estimate=pl.CostEstimate(flops=3_200_000_000, bytes_accessed=14_000_000, transcendentals=700_000),
        name="forward",
    )(place, mine, other, x0, tiles, parents_fine, nb_mid, parents_mid)


def sign_smooth(v):
    return v * lax.rsqrt(v * v + SMOOTH)


def backward_kernel(
    cohort_ref, own_ref, obs_ref, w_ref, tiles_mid_ref, slope2_ref, x2_ref, slope1_ref, x_ref, tiles_ref,
    parents_ref, nb_mid_ref, parents_mid_ref, out_ref, g1_ref,
):
    j = pl.program_id(0)

    def put(piece, half, lanes, value):
        for z in range(4):
            for y in range(4):
                row = (z * 4 + y) * 16
                out_ref[lax.rem(piece, 2), lax.div(piece, 2), y, z, :, pl.ds(half, lanes)] = value[row : row + 16].astype(bf16)

    @pl.when(j == 0)
    def _():
        own = own_ref[...]
        spread = jnp.zeros_like(own)
        for peer in range(MEMBERS // LOCAL):
            theirs = cohort_ref[peer]
            spread = spread + sign_smooth(own - theirs) + sign_smooth(own - pltpu.roll(theirs, CELLS_OUT, 1))
        skill = sign_smooth(own - obs_ref[...])
        slope = NORM * (skill / MEMBERS - spread / (MEMBERS * (MEMBERS - 1)))
        slope = jnp.concatenate([slope, jnp.zeros((128 - FIELD_ROWS, 128), f32)], 0).astype(bf16)
        put(7, 0, 128, dot_bt(x2_ref[...], slope))
        put(7, 128, PIECE - 128, jnp.zeros((CHANNELS, PIECE - 128), f32))
        pool = one_hot(parents_mid_ref[...], CELLS_OUT)
        head_t = w_ref[:, HEAD_AT : HEAD_AT + 128]
        dh2, g2 = [], []
        for i in range(LOCAL):
            wide = dot(slope[:, i * CELLS_OUT : (i + 1) * CELLS_OUT], pool).astype(bf16)
            dh2.append(dot(head_t, wide) * 0.25)
            g2.append((dh2[i] * slope2_ref[i]).astype(bf16))
        for q in range(SLOTS):
            rows = slice(q * CHANNELS, (q + 1) * CHANNELS)
            grad = dot_bt(g2[0], tiles_mid_ref[0, rows]) + dot_bt(g2[1], tiles_mid_ref[1, rows])
            put((SLOTS + q) // 2, (SLOTS + q) % 2 * 256, 256, grad)
        both = jnp.concatenate(g2, 0)
        back = [dh2[i] + dot_at(w_ref[:, SECOND_AT : SECOND_AT + CHANNELS], g2[i]) for i in range(LOCAL)]
        for q in range(1, SLOTS):
            spread_back = dot_bt(both, one_hot(nb_mid_ref[q : q + 1, :], CELLS_MID)).astype(bf16)
            weight = w_ref[:, SECOND_AT + q * CHANNELS : SECOND_AT + (q + 1) * CHANNELS]
            for i in range(LOCAL):
                back[i] = back[i] + dot_at(weight, spread_back[i * CHANNELS : (i + 1) * CHANNELS])
        unpool = one_hot(parents_ref[...], CELLS_MID)
        for i in range(LOCAL):
            dh1 = dot((back[i] * 0.25).astype(bf16), unpool)
            g1_ref[i] = (dh1 * slope1_ref[i].astype(f32)).astype(bf16)
        put(0, 0, 256, dot_bt(g1_ref[0], x_ref[0]) + dot_bt(g1_ref[1], x_ref[1]))

    @pl.when(j > 0)
    def _():
        grad = dot_bt(g1_ref[0], tiles_ref[0, 0]) + dot_bt(g1_ref[1], tiles_ref[1, 0])
        put(lax.div(j, 2), pl.multiple_of(lax.rem(j, 2) * 256, 256), 256, grad)


def backward(cohort, own, obs, w, tiles_mid, slope2, x2, slope1, x0, tiles, parents_fine, nb_mid, parents_mid):
    whole = lambda *shape: pl.BlockSpec(shape, lambda j: (0,) * len(shape))
    return pl.pallas_call(
        backward_kernel,
        grid=(SLOTS,),
        in_specs=[
            whole(*cohort.shape), whole(*own.shape), whole(*obs.shape), whole(*w.shape), whole(*tiles_mid.shape),
            whole(*slope2.shape), whole(*x2.shape), whole(*slope1.shape), whole(*x0.shape),
            pl.BlockSpec((LOCAL, 1, CHANNELS, CELLS_IN), lambda j: (0, jnp.maximum(j - 1, 0), 0, 0)),
            whole(*parents_fine.shape), whole(*nb_mid.shape), whole(*parents_mid.shape),
        ],
        out_specs=whole(2, 4, 4, 4, 16, PIECE),
        out_shape=jax.ShapeDtypeStruct((2, 4, 4, 4, 16, PIECE), bf16),
        scratch_shapes=[pltpu.VMEM((LOCAL, CHANNELS, CELLS_IN), bf16)],
        compiler_params=pltpu.CompilerParams(vmem_limit_bytes=VMEM_BYTES),
        cost_estimate=pl.CostEstimate(flops=4_000_000_000, bytes_accessed=16_000_000, transcendentals=200_000),
        name="backward",
    )(cohort, own, obs, w, tiles_mid, slope2, x2, slope1, x0, tiles, parents_fine, nb_mid, parents_mid)


def shift(v, axis, n, by):
    return lax.ppermute(v, axis, [(i, (i + by) % n) for i in range(n)])


def gather_weights(weight_first, weight_second, weight_head, core, x):
    rows = weight_first.shape[1]
    flat = jnp.concatenate(
        [
            weight_first.transpose(1, 0, 2).reshape(rows, SECOND_AT),
            weight_second.transpose(1, 0, 2).reshape(rows, SECOND_AT),
            weight_head.T,
            jnp.zeros((rows, WIDTH - HEAD_AT - FIELDS), bf16),
        ],
        1,
    )
    pair = lax.dynamic_slice_in_dim(flat, x * 2 * PIECE, 2 * PIECE, 1)
    kept = lax.dynamic_slice_in_dim(pair, core * PIECE, PIECE, 1)
    sent = lax.dynamic_slice_in_dim(pair, (1 - core) * PIECE, PIECE, 1)
    came = shift(sent, "core", 2, 1)
    mine = jnp.where(core == 0, jnp.concatenate([kept, came], 0), jnp.concatenate([came, kept], 0))
    column = jnp.stack([mine] + [shift(mine, "z_hi", 4, s) for s in (1, 2, 3)])
    plane = lax.all_to_all(jnp.broadcast_to(column, (16,) + column.shape), ("x", "y"), 0, 0)
    return plane, shift(plane, "core", 2, 1)


def reduce_gradients(parts, core, x):
    kept = lax.dynamic_index_in_dim(parts, core, 0, keepdims=False)
    sent = lax.dynamic_index_in_dim(parts, 1 - core, 0, keepdims=False)
    total = (kept.astype(f32) + shift(sent, "core", 2, 1).astype(f32)).astype(bf16)
    plane = lax.all_to_all(total.reshape(16, 4, 16, PIECE), ("x", "y"), 0, 0)
    total = jnp.sum(plane.astype(f32), 0).astype(bf16)
    column = jnp.broadcast_to(total[:, None], (4, 2, 16, PIECE)).reshape(8, 16, PIECE)
    column = lax.all_to_all(column, ("z_hi", "z_lo"), 0, 0)
    total = jnp.sum(column.astype(f32), 0).astype(bf16).reshape(2, 8, PIECE)
    kept = lax.dynamic_index_in_dim(total, core, 0, keepdims=False)
    came = shift(lax.dynamic_index_in_dim(total, 1 - core, 0, keepdims=False), "core", 2, 1)
    pair = jnp.where(core == 0, jnp.concatenate([kept, came], 1), jnp.concatenate([came, kept], 1))
    back = [pair] + [shift(pair, "x", 4, s) for s in (1, 2, 3)]
    ring = jnp.stack([back[i] for i in (3, 2, 1, 0, 3, 2, 1)])
    return lax.dynamic_slice_in_dim(ring, 3 - x, 4, 0).astype(f32).transpose(1, 0, 2).reshape(8, WIDTH)


def per_device(
    member_fields, weight_first, weight_second, weight_head,
    neighbours_fine, neighbours_mid, parents_fine, parents_mid, observations,
):
    core, x = lax.axis_index("core"), lax.axis_index("x")
    place = jnp.stack([core, lax.axis_index("z_hi")]).astype(jnp.int32)
    x0 = member_fields[0]
    parents_fine = parents_fine.reshape(1, CELLS_IN)
    parents_mid = parents_mid.reshape(1, CELLS_MID)
    truth = jnp.pad(observations[0], ((0, FIELD_ROWS - FIELDS), (0, 0)))
    truth = jnp.concatenate([truth] * LOCAL, 1)

    mine, other = gather_weights(weight_first, weight_second, weight_head, core, x)
    tiles = fine_tiles(x0.reshape(LOCAL * CHANNELS, CELLS_IN), neighbours_fine[1:].reshape(SLOTS - 1, 1, CELLS_IN))
    slope1, w, tiles_mid, slope2, x2, pred = forward(
        place, mine, other, x0, tiles, parents_fine, neighbours_mid, parents_mid
    )
    cohort = lax.all_to_all(jnp.broadcast_to(pred, (MEMBERS // LOCAL,) + pred.shape), MEM, 0, 0)
    parts = backward(
        cohort, pred, truth, w, tiles_mid, slope2, x2, slope1, x0, tiles, parents_fine, neighbours_mid, parents_mid
    )
    rows = reduce_gradients(parts, core, x)
    return (
        rows[:, :SECOND_AT].reshape(8, SLOTS, CHANNELS).transpose(1, 0, 2),
        rows[:, SECOND_AT:HEAD_AT].reshape(8, SLOTS, CHANNELS).transpose(1, 0, 2),
        rows[:, HEAD_AT : HEAD_AT + FIELDS].T,
    )


def solution(mesh):
    fine_mesh = Mesh(mesh.devices.reshape(2, 4, 4, 4, 2), ("z_lo", "x", "z_hi", "y", "core"))
    placed = (
        P(DP, MEM, None, None),
        P(None, DP, None),
        P(None, DP, None),
        P(None, DP),
        P(),
        P(),
        P(),
        P(),
        P(DP, None, None),
    )
    return jax.shard_map(
        per_device,
        mesh=fine_mesh,
        in_specs=placed,
        out_specs=(P(None, DP, None), P(None, DP, None), P(None, DP)),
        check_vma=False,
    )
```

```python
import math

import jax
import jax.numpy as jnp
from jax import lax
from jax.experimental import pallas as pl
from jax.experimental.pallas import tpu as pltpu
from jax.sharding import Mesh
from jax.sharding import PartitionSpec as P

DP = ("z_hi", "y", "core")
MEM = ("z_lo", "x")

MEMBERS = 16
CHANNELS = 256
SLOTS = 7
FIELDS = 69
FIELD_ROWS = 72
CELLS_OUT = 64
CELLS_MID = 256
CELLS_IN = 1024
SAMPLES = 32
LOCAL = 2
QUARTER = 1024
SMOOTH = 0.0001
NORM = MEMBERS / math.sqrt(SAMPLES * CELLS_OUT)
SECOND_AT = SLOTS * CHANNELS
HEAD_AT = 2 * SLOTS * CHANNELS
WIDTH = 4096
MIB = 1024 * 1024

f32 = jnp.float32
bf16 = jnp.bfloat16


def dot(a, b):
    return lax.dot_general(a, b, (((1,), (0,)), ((), ())), preferred_element_type=f32)


def dot_bt(a, b):
    return lax.dot_general(a, b, (((1,), (1,)), ((), ())), preferred_element_type=f32)


def dot_at(a, b):
    return lax.dot_general(a, b, (((0,), (0,)), ((), ())), preferred_element_type=f32)


def one_hot(index_row, rows):
    shape = (rows, index_row.shape[1])
    return jnp.where(lax.broadcasted_iota(jnp.int32, shape, 0) == index_row, 1.0, 0.0).astype(bf16)


def tiles_kernel(x_ref, nb_ref, out_ref):
    row = nb_ref[pl.ds(pl.program_id(0) + 1, 1), :]
    tile = dot(x_ref[...], one_hot(row, CELLS_IN)).astype(bf16)
    for m in range(LOCAL):
        out_ref[m, 0] = tile[m * CHANNELS : (m + 1) * CHANNELS]


def fine_tiles(x0, nb):
    return pl.pallas_call(
        tiles_kernel,
        grid=(SLOTS - 1,),
        in_specs=[
            pl.BlockSpec((LOCAL * CHANNELS, CELLS_IN), lambda j: (0, 0)),
            pl.BlockSpec((SLOTS, CELLS_IN), lambda j: (0, 0)),
        ],
        out_specs=pl.BlockSpec((LOCAL, 1, CHANNELS, CELLS_IN), lambda j: (0, j, 0, 0)),
        out_shape=jax.ShapeDtypeStruct((LOCAL, SLOTS - 1, CHANNELS, CELLS_IN), bf16),
        compiler_params=pltpu.CompilerParams(vmem_limit_bytes=56 * MIB),
        cost_estimate=pl.CostEstimate(flops=6_500_000_000, bytes_accessed=8_000_000, transcendentals=0),
        name="fine_tiles",
    )(x0, nb)


def forward_kernel(
    place_ref, mine_ref, other_ref, x_ref, tiles_ref, parents_ref, nb_mid_ref, parents_mid_ref,
    slope1_ref, w_ref, tiles_mid_ref, slope2_ref, x2_ref, pred_ref, pooled_ref,
):
    m, k = pl.program_id(0), pl.program_id(1)

    @pl.when((m == 0) & (k == 0))
    def _():
        first, z = place_ref[0] == 0, place_ref[1]
        for x in range(4):
            for y in range(4):
                for back in range(4):
                    mine, other = mine_ref[x * 4 + y, back].astype(f32), other_ref[x * 4 + y, back].astype(f32)
                    pair = jnp.concatenate([jnp.where(first, mine, other), jnp.where(first, other, mine)], 0)
                    row = pl.multiple_of((lax.rem(z - back + 4, 4) * 4 + y) * 16, 16)
                    w_ref[pl.ds(row, 16), x * QUARTER : (x + 1) * QUARTER] = pair.astype(bf16)

    a1 = dot(w_ref[:, 0:CHANNELS], x_ref[0])
    for j in range(1, SLOTS):
        a1 = a1 + dot(w_ref[:, j * CHANNELS : (j + 1) * CHANNELS], tiles_ref[0, j - 1])
    gate = jax.nn.sigmoid(a1)
    slope1_ref[0] = (gate * (1.0 + a1 * (1.0 - gate))).astype(bf16)
    h1 = (x_ref[0].astype(f32) + a1 * gate).astype(bf16)
    part = dot_bt(h1, one_hot(parents_ref[...], CELLS_MID))

    @pl.when(k == 0)
    def _():
        pooled_ref[m] = part

    @pl.when(k > 0)
    def _():
        pooled_ref[m] += part

    @pl.when((m == LOCAL - 1) & (k == pl.num_programs(1) - 1))
    def _():
        x1 = (pooled_ref[...].reshape(LOCAL * CHANNELS, CELLS_MID) * 0.25).astype(bf16)
        for i in range(LOCAL):
            tiles_mid_ref[i, 0:CHANNELS] = x1[i * CHANNELS : (i + 1) * CHANNELS]
        for j in range(1, SLOTS):
            tile = dot(x1, one_hot(nb_mid_ref[j : j + 1, :], CELLS_MID)).astype(bf16)
            for i in range(LOCAL):
                tiles_mid_ref[i, j * CHANNELS : (j + 1) * CHANNELS] = tile[i * CHANNELS : (i + 1) * CHANNELS]
        pool = one_hot(parents_mid_ref[...], CELLS_OUT)
        for i in range(LOCAL):
            a2 = dot(w_ref[:, SECOND_AT:HEAD_AT], tiles_mid_ref[i])
            gate2 = jax.nn.sigmoid(a2)
            slope2_ref[i] = gate2 * (1.0 + a2 * (1.0 - gate2))
            h2 = (x1[i * CHANNELS : (i + 1) * CHANNELS].astype(f32) + a2 * gate2).astype(bf16)
            x2_ref[:, i * CELLS_OUT : (i + 1) * CELLS_OUT] = (dot_bt(h2, pool) * 0.25).astype(bf16)
        pred = dot_at(w_ref[:, HEAD_AT : HEAD_AT + 128], x2_ref[...])
        pred_ref[...] = pred[0:FIELD_ROWS]


def spread_kernel(own_ref, back1_ref, back2_ref, back3_ref, out_ref):
    for block in range(16):
        for back, source in enumerate((own_ref, back1_ref, back2_ref, back3_ref)):
            out_ref[block, back] = source[...]


def spread(pieces):
    return pl.pallas_call(
        spread_kernel,
        in_specs=[pl.BlockSpec(memory_space=pltpu.VMEM)] * 4,
        out_specs=pl.BlockSpec(memory_space=pltpu.VMEM),
        out_shape=jax.ShapeDtypeStruct((16, 4, 8, QUARTER), bf16),
        compiler_params=pltpu.CompilerParams(vmem_limit_bytes=8 * MIB),
        name="spread",
    )(*pieces)


def after_kernel(value_ref, first_ref, out_ref):
    del value_ref, first_ref, out_ref


def after(value, first):
    return pl.pallas_call(
        after_kernel,
        in_specs=[pl.BlockSpec(memory_space=pl.ANY)] * 2,
        out_specs=pl.BlockSpec(memory_space=pl.ANY),
        out_shape=jax.ShapeDtypeStruct(value.shape, value.dtype),
        input_output_aliases={0: 0},
        compiler_params=pltpu.CompilerParams(vmem_limit_bytes=48 * MIB),
        name="after",
    )(value, first)


def forward(place, mine, other, x0, tiles, parents_fine, nb_mid, parents_mid):
    chunk = 256
    whole = lambda *shape: pl.BlockSpec(shape, lambda m, k: (0,) * len(shape))
    return pl.pallas_call(
        forward_kernel,
        grid=(LOCAL, CELLS_IN // chunk),
        in_specs=[
            pl.BlockSpec(memory_space=pltpu.SMEM),
            whole(16, 4, 8, QUARTER),
            whole(16, 4, 8, QUARTER),
            pl.BlockSpec((1, CHANNELS, chunk), lambda m, k: (m, 0, k)),
            pl.BlockSpec((1, SLOTS - 1, CHANNELS, chunk), lambda m, k: (m, 0, 0, k)),
            pl.BlockSpec((1, chunk), lambda m, k: (0, k)),
            whole(SLOTS, CELLS_MID),
            whole(1, CELLS_MID),
        ],
        out_specs=[
            pl.BlockSpec((1, CHANNELS, chunk), lambda m, k: (m, 0, k)),
            whole(CHANNELS, WIDTH),
            whole(LOCAL, SECOND_AT, CELLS_MID),
            whole(LOCAL, CHANNELS, CELLS_MID),
            whole(CHANNELS, LOCAL * CELLS_OUT),
            whole(FIELD_ROWS, LOCAL * CELLS_OUT),
        ],
        out_shape=[
            pltpu.HBM((LOCAL, CHANNELS, CELLS_IN), bf16),
            pltpu.HBM((CHANNELS, WIDTH), bf16),
            pltpu.HBM((LOCAL, SECOND_AT, CELLS_MID), bf16),
            pltpu.HBM((LOCAL, CHANNELS, CELLS_MID), f32),
            jax.ShapeDtypeStruct((CHANNELS, LOCAL * CELLS_OUT), bf16),
            jax.ShapeDtypeStruct((FIELD_ROWS, LOCAL * CELLS_OUT), f32),
        ],
        scratch_shapes=[pltpu.VMEM((LOCAL, CHANNELS, CELLS_MID), f32)],
        compiler_params=pltpu.CompilerParams(vmem_limit_bytes=48 * MIB),
        cost_estimate=pl.CostEstimate(flops=3_200_000_000, bytes_accessed=14_000_000, transcendentals=700_000),
        name="forward",
    )(place, mine, other, x0, tiles, parents_fine, nb_mid, parents_mid)


def sign_smooth(v):
    return v * lax.rsqrt(v * v + SMOOTH)


def backward_kernel(
    place_ref, cohort0_ref, cohort1_ref, cohort2_ref, cohort3_ref, own_ref, obs_ref, w_ref, tiles_mid_ref, slope2_ref, x2_ref, slope1_ref, x_ref, tiles_ref,
    parents_ref, nb_mid_ref, parents_mid_ref, kept_ref, sent_ref, g1_ref,
):
    j = pl.program_id(0)
    first = place_ref[0] == 0
    cohort_refs = (cohort0_ref, cohort1_ref, cohort2_ref, cohort3_ref)

    def put(quarter, at, lanes, value):
        for z in range(4):
            for y in range(4):
                row = (z * 4 + y) * 16
                low, high = value[row : row + 8], value[row + 8 : row + 16]
                kept_ref[quarter, y, z, :, pl.ds(at, lanes)] = jnp.where(first, low, high).astype(bf16)
                sent_ref[quarter, y, z, :, pl.ds(at, lanes)] = jnp.where(first, high, low).astype(bf16)

    @pl.when(j == 0)
    def _():
        own = own_ref[...]
        spread = jnp.zeros_like(own)
        for pair_ref in cohort_refs:
            for peer in range(2):
                theirs = pair_ref[peer]
                spread = spread + sign_smooth(own - theirs) + sign_smooth(own - pltpu.roll(theirs, CELLS_OUT, 1))
        skill = sign_smooth(own - obs_ref[...])
        slope = NORM * (skill / MEMBERS - spread / (MEMBERS * (MEMBERS - 1)))
        slope = jnp.concatenate([slope, jnp.zeros((128 - FIELD_ROWS, 128), f32)], 0).astype(bf16)
        put(3, 512, 128, dot_bt(x2_ref[...], slope))
        put(3, 640, 384, jnp.zeros((CHANNELS, 384), f32))
        pool = one_hot(parents_mid_ref[...], CELLS_OUT)
        head_t = w_ref[:, HEAD_AT : HEAD_AT + 128]
        dh2, g2 = [], []
        for i in range(LOCAL):
            wide = dot(slope[:, i * CELLS_OUT : (i + 1) * CELLS_OUT], pool).astype(bf16)
            dh2.append(dot(head_t, wide) * 0.25)
            g2.append((dh2[i] * slope2_ref[i]).astype(bf16))
        for q in range(SLOTS):
            rows = slice(q * CHANNELS, (q + 1) * CHANNELS)
            grad = dot_bt(g2[0], tiles_mid_ref[0, rows]) + dot_bt(g2[1], tiles_mid_ref[1, rows])
            put((SLOTS + q) // 4, (SLOTS + q) % 4 * 256, 256, grad)
        both = jnp.concatenate(g2, 0)
        back = [dh2[i] + dot_at(w_ref[:, SECOND_AT : SECOND_AT + CHANNELS], g2[i]) for i in range(LOCAL)]
        for q in range(1, SLOTS):
            spread_back = dot_bt(both, one_hot(nb_mid_ref[q : q + 1, :], CELLS_MID)).astype(bf16)
            weight = w_ref[:, SECOND_AT + q * CHANNELS : SECOND_AT + (q + 1) * CHANNELS]
            for i in range(LOCAL):
                back[i] = back[i] + dot_at(weight, spread_back[i * CHANNELS : (i + 1) * CHANNELS])
        unpool = one_hot(parents_ref[...], CELLS_MID)
        for i in range(LOCAL):
            dh1 = dot((back[i] * 0.25).astype(bf16), unpool)
            g1_ref[i] = (dh1 * slope1_ref[i].astype(f32)).astype(bf16)
        put(0, 0, 256, dot_bt(g1_ref[0], x_ref[0]) + dot_bt(g1_ref[1], x_ref[1]))

    @pl.when(j > 0)
    def _():
        grad = dot_bt(g1_ref[0], tiles_ref[0, 0]) + dot_bt(g1_ref[1], tiles_ref[1, 0])
        put(lax.div(j, 4), pl.multiple_of(lax.rem(j, 4) * 256, 256), 256, grad)


def backward(place, cohort, own, obs, w, tiles_mid, slope2, x2, slope1, x0, tiles, parents_fine, nb_mid, parents_mid):
    whole = lambda *shape: pl.BlockSpec(shape, lambda j: (0,) * len(shape))
    return pl.pallas_call(
        backward_kernel,
        grid=(SLOTS,),
        in_specs=[
            pl.BlockSpec(memory_space=pltpu.SMEM), *[whole(*pair.shape) for pair in cohort], whole(*own.shape), whole(*obs.shape), whole(*w.shape), whole(*tiles_mid.shape),
            whole(*slope2.shape), whole(*x2.shape), whole(*slope1.shape), whole(*x0.shape),
            pl.BlockSpec((LOCAL, 1, CHANNELS, CELLS_IN), lambda j: (0, jnp.maximum(j - 1, 0), 0, 0)),
            whole(*parents_fine.shape), whole(*nb_mid.shape), whole(*parents_mid.shape),
        ],
        out_specs=[whole(4, 4, 4, 8, QUARTER)] * 2,
        out_shape=[jax.ShapeDtypeStruct((4, 4, 4, 8, QUARTER), bf16)] * 2,
        scratch_shapes=[pltpu.VMEM((LOCAL, CHANNELS, CELLS_IN), bf16)],
        compiler_params=pltpu.CompilerParams(vmem_limit_bytes=50 * MIB),
        cost_estimate=pl.CostEstimate(flops=4_000_000_000, bytes_accessed=16_000_000, transcendentals=200_000),
        name="backward",
    )(place, *cohort, own, obs, w, tiles_mid, slope2, x2, slope1, x0, tiles, parents_fine, nb_mid, parents_mid)


def shift(v, axis, n, by):
    return lax.ppermute(v, axis, [(i, (i + by) % n) for i in range(n)])


def gather_weights(weight_first, weight_second, weight_head, x, tiles):
    rows = weight_first.shape[1]
    flat = jnp.concatenate(
        [
            weight_first.transpose(1, 0, 2).reshape(rows, SECOND_AT),
            weight_second.transpose(1, 0, 2).reshape(rows, SECOND_AT),
            weight_head.T,
            jnp.zeros((rows, WIDTH - HEAD_AT - FIELDS), bf16),
        ],
        1,
    )
    mine = lax.dynamic_slice_in_dim(flat, x * QUARTER, QUARTER, 1)
    column = spread([mine] + [shift(mine, "z_hi", 4, s) for s in (1, 2, 3)])
    plane = after(lax.all_to_all(column, ("x", "y"), 0, 0), tiles)
    return plane, shift(plane, "core", 2, 1)


def reduce_gradients(kept, sent, x):
    total = (kept.astype(f32) + shift(sent, "core", 2, 1).astype(f32)).astype(bf16)
    plane = lax.all_to_all(total.reshape(16, 4, 8, QUARTER), ("x", "y"), 0, 0)
    total = jnp.sum(plane.astype(f32), 0).astype(bf16)
    column = jnp.broadcast_to(total[:, None], (4, 2, 8, QUARTER)).reshape(8, 8, QUARTER)
    column = lax.all_to_all(column, ("z_hi", "z_lo"), 0, 0)
    total = jnp.sum(column.astype(f32), 0).astype(bf16)
    back = [total] + [shift(total, "x", 4, s) for s in (1, 2, 3)]
    ring = jnp.stack([back[i] for i in (3, 2, 1, 0, 3, 2, 1)])
    return lax.dynamic_slice_in_dim(ring, 3 - x, 4, 0).astype(f32).transpose(1, 0, 2).reshape(8, WIDTH)


def per_device(
    member_fields, weight_first, weight_second, weight_head,
    neighbours_fine, neighbours_mid, parents_fine, parents_mid, observations,
):
    core, x = lax.axis_index("core"), lax.axis_index("x")
    place = jnp.stack([core, lax.axis_index("z_hi")]).astype(jnp.int32)
    x0 = member_fields[0]
    parents_fine = parents_fine.reshape(1, CELLS_IN)
    parents_mid = parents_mid.reshape(1, CELLS_MID)
    truth = jnp.pad(observations[0], ((0, FIELD_ROWS - FIELDS), (0, 0)))
    truth = jnp.concatenate([truth] * LOCAL, 1)

    tiles = fine_tiles(x0.reshape(LOCAL * CHANNELS, CELLS_IN), neighbours_fine)
    mine, other = gather_weights(weight_first, weight_second, weight_head, x, tiles)
    slope1, w, tiles_mid, slope2, x2, pred = forward(
        place, mine, other, x0, tiles, parents_fine, neighbours_mid, parents_mid
    )
    pair = jnp.stack([pred, shift(pred, "z_lo", 2, 1)])
    cohort = [pair] + [shift(pair, "x", 4, s) for s in (1, 2, 3)]
    kept, sent = backward(
        place, cohort, pred, truth, w, tiles_mid, slope2, x2, slope1, x0, tiles, parents_fine, neighbours_mid, parents_mid
    )
    rows = reduce_gradients(kept, sent, x)
    return (
        rows[:, :SECOND_AT].reshape(8, SLOTS, CHANNELS).transpose(1, 0, 2),
        rows[:, SECOND_AT:HEAD_AT].reshape(8, SLOTS, CHANNELS).transpose(1, 0, 2),
        rows[:, HEAD_AT : HEAD_AT + FIELDS].T,
    )


def solution(mesh):
    fine_mesh = Mesh(mesh.devices.reshape(2, 4, 4, 4, 2), ("z_lo", "x", "z_hi", "y", "core"))
    placed = (
        P(DP, MEM, None, None),
        P(None, DP, None),
        P(None, DP, None),
        P(None, DP),
        P(),
        P(),
        P(),
        P(),
        P(DP, None, None),
    )
    return jax.shard_map(
        per_device,
        mesh=fine_mesh,
        in_specs=placed,
        out_specs=(P(None, DP, None), P(None, DP, None), P(None, DP)),
        check_vma=False,
    )
```

```python
import math

import jax
import jax.numpy as jnp
from jax import lax
from jax.experimental import pallas as pl
from jax.experimental.pallas import tpu as pltpu
from jax.sharding import Mesh
from jax.sharding import PartitionSpec as P

DP = ("z_hi", "y", "core")
MEM = ("z_lo", "x")

MEMBERS = 16
CHANNELS = 256
SLOTS = 7
FIELDS = 69
FIELD_ROWS = 72
CELLS_OUT = 64
CELLS_MID = 256
CELLS_IN = 1024
SAMPLES = 32
LOCAL = 2
QUARTER = 1024
SMOOTH = 0.0001
NORM = MEMBERS / math.sqrt(SAMPLES * CELLS_OUT)
SECOND_AT = SLOTS * CHANNELS
HEAD_AT = 2 * SLOTS * CHANNELS
WIDTH = 4096
MIB = 1024 * 1024

f32 = jnp.float32
bf16 = jnp.bfloat16


def dot(a, b):
    return lax.dot_general(a, b, (((1,), (0,)), ((), ())), preferred_element_type=f32)


def dot_bt(a, b):
    return lax.dot_general(a, b, (((1,), (1,)), ((), ())), preferred_element_type=f32)


def dot_at(a, b):
    return lax.dot_general(a, b, (((0,), (0,)), ((), ())), preferred_element_type=f32)


def one_hot(index_row, rows):
    shape = (rows, index_row.shape[1])
    return jnp.where(lax.broadcasted_iota(jnp.int32, shape, 0) == index_row, 1.0, 0.0).astype(bf16)


def tiles_kernel(x_ref, nb_ref, out_ref):
    row = nb_ref[pl.ds(pl.program_id(0) + 1, 1), :]
    tile = dot(x_ref[...], one_hot(row, CELLS_IN)).astype(bf16)
    for m in range(LOCAL):
        out_ref[m, 0] = tile[m * CHANNELS : (m + 1) * CHANNELS]


def fine_tiles(x0, nb):
    return pl.pallas_call(
        tiles_kernel,
        grid=(SLOTS - 1,),
        in_specs=[
            pl.BlockSpec((LOCAL * CHANNELS, CELLS_IN), lambda j: (0, 0)),
            pl.BlockSpec((SLOTS, CELLS_IN), lambda j: (0, 0)),
        ],
        out_specs=pl.BlockSpec((LOCAL, 1, CHANNELS, CELLS_IN), lambda j: (0, j, 0, 0)),
        out_shape=jax.ShapeDtypeStruct((LOCAL, SLOTS - 1, CHANNELS, CELLS_IN), bf16),
        compiler_params=pltpu.CompilerParams(vmem_limit_bytes=56 * MIB),
        cost_estimate=pl.CostEstimate(flops=6_500_000_000, bytes_accessed=8_000_000, transcendentals=0),
        name="fine_tiles",
    )(x0, nb)


def forward_kernel(
    place_ref, mine_ref, other_ref, x_ref, parents_ref, nb_mid_ref, parents_mid_ref, tiles_hbm,
    x2_ref, pred_ref, slope1_hbm, w_hbm, tiles_mid_hbm, slope2_hbm,
    tiles_ref, w_ref, slope1_ref, tiles_mid_ref, slope2_ref, in_sem, out_sem,
):
    loads = [pltpu.make_async_copy(tiles_hbm.at[m], tiles_ref.at[m], in_sem.at[m]) for m in range(LOCAL)]
    for load in loads:
        load.start()
    first, z = place_ref[0] == 0, place_ref[1]
    for x in range(4):
        for y in range(4):
            for back in range(4):
                mine, other = mine_ref[x * 4 + y, back].astype(f32), other_ref[x * 4 + y, back].astype(f32)
                pair = jnp.concatenate([jnp.where(first, mine, other), jnp.where(first, other, mine)], 0)
                row = pl.multiple_of((lax.rem(z - back + 4, 4) * 4 + y) * 16, 16)
                w_ref[pl.ds(row, 16), x * QUARTER : (x + 1) * QUARTER] = pair.astype(bf16)
    stores = [pltpu.make_async_copy(w_ref.at[:, SECOND_AT : HEAD_AT + 128], w_hbm, out_sem.at[0])]
    stores[0].start()
    unpool = one_hot(parents_ref[...], CELLS_MID)
    x1 = []
    for m in range(LOCAL):
        loads[m].wait()
        pooled = jnp.zeros((CHANNELS, CELLS_MID), f32)
        for at in range(0, CELLS_IN, 512):
            cells = slice(at, at + 512)
            a1 = dot(w_ref[:, 0:CHANNELS], x_ref[m, :, cells])
            for j in range(1, SLOTS):
                a1 = a1 + dot(w_ref[:, j * CHANNELS : (j + 1) * CHANNELS], tiles_ref[m, j - 1, :, cells])
            gate = jax.nn.sigmoid(a1)
            slope1_ref[m, :, cells] = (gate * (1.0 + a1 * (1.0 - gate))).astype(bf16)
            h1 = (x_ref[m, :, cells].astype(f32) + a1 * gate).astype(bf16)
            pooled = pooled + dot_bt(h1, unpool[:, cells])
        stores.append(pltpu.make_async_copy(slope1_ref.at[m], slope1_hbm.at[m], out_sem.at[1 + m]))
        stores[-1].start()
        x1.append((pooled * 0.25).astype(bf16))
        tiles_mid_ref[m, 0:CHANNELS] = x1[m]
    both = jnp.concatenate(x1, 0)
    for j in range(1, SLOTS):
        tile = dot(both, one_hot(nb_mid_ref[j : j + 1, :], CELLS_MID)).astype(bf16)
        for m in range(LOCAL):
            tiles_mid_ref[m, j * CHANNELS : (j + 1) * CHANNELS] = tile[m * CHANNELS : (m + 1) * CHANNELS]
    stores.append(pltpu.make_async_copy(tiles_mid_ref, tiles_mid_hbm, out_sem.at[3]))
    stores[-1].start()
    pool = one_hot(parents_mid_ref[...], CELLS_OUT)
    for m in range(LOCAL):
        a2 = dot(w_ref[:, SECOND_AT:HEAD_AT], tiles_mid_ref[m])
        gate2 = jax.nn.sigmoid(a2)
        slope2_ref[m] = gate2 * (1.0 + a2 * (1.0 - gate2))
        h2 = (x1[m].astype(f32) + a2 * gate2).astype(bf16)
        x2_ref[:, m * CELLS_OUT : (m + 1) * CELLS_OUT] = (dot_bt(h2, pool) * 0.25).astype(bf16)
    stores.append(pltpu.make_async_copy(slope2_ref, slope2_hbm, out_sem.at[4]))
    stores[-1].start()
    pred = dot_at(w_ref[:, HEAD_AT : HEAD_AT + 128], x2_ref[...])
    pred_ref[...] = pred[0:FIELD_ROWS]
    for store in stores:
        store.wait()


def spread_kernel(own_ref, back1_ref, back2_ref, back3_ref, out_ref):
    for block in range(16):
        for back, source in enumerate((own_ref, back1_ref, back2_ref, back3_ref)):
            out_ref[block, back] = source[...]


def spread(pieces):
    return pl.pallas_call(
        spread_kernel,
        in_specs=[pl.BlockSpec(memory_space=pltpu.VMEM)] * 4,
        out_specs=pl.BlockSpec(memory_space=pltpu.VMEM),
        out_shape=jax.ShapeDtypeStruct((16, 4, 8, QUARTER), bf16),
        compiler_params=pltpu.CompilerParams(vmem_limit_bytes=8 * MIB),
        name="spread",
    )(*pieces)


def after_kernel(value_ref, first_ref, out_ref):
    del value_ref, first_ref, out_ref


def after(value, first):
    return pl.pallas_call(
        after_kernel,
        in_specs=[pl.BlockSpec(memory_space=pl.ANY)] * 2,
        out_specs=pl.BlockSpec(memory_space=pl.ANY),
        out_shape=jax.ShapeDtypeStruct(value.shape, value.dtype),
        input_output_aliases={0: 0},
        compiler_params=pltpu.CompilerParams(vmem_limit_bytes=48 * MIB),
        name="after",
    )(value, first)


VMEM = pl.BlockSpec(memory_space=pltpu.VMEM)
HBM = pl.BlockSpec(memory_space=pltpu.HBM)
SMEM = pl.BlockSpec(memory_space=pltpu.SMEM)
TILES = (LOCAL, SLOTS - 1, CHANNELS, CELLS_IN)
BACK_W = SECOND_AT + 128


def forward(place, mine, other, x0, tiles, parents_fine, nb_mid, parents_mid):
    return pl.pallas_call(
        forward_kernel,
        in_specs=[SMEM, VMEM, VMEM, VMEM, VMEM, VMEM, VMEM, HBM],
        out_specs=[VMEM, VMEM, HBM, HBM, HBM, HBM],
        out_shape=[
            jax.ShapeDtypeStruct((CHANNELS, LOCAL * CELLS_OUT), bf16),
            jax.ShapeDtypeStruct((FIELD_ROWS, LOCAL * CELLS_OUT), f32),
            pltpu.HBM((LOCAL, CHANNELS, CELLS_IN), bf16),
            pltpu.HBM((CHANNELS, BACK_W), bf16),
            pltpu.HBM((LOCAL, SECOND_AT, CELLS_MID), bf16),
            pltpu.HBM((LOCAL, CHANNELS, CELLS_MID), f32),
        ],
        scratch_shapes=[
            pltpu.VMEM(TILES, bf16),
            pltpu.VMEM((CHANNELS, WIDTH), bf16),
            pltpu.VMEM((LOCAL, CHANNELS, CELLS_IN), bf16),
            pltpu.VMEM((LOCAL, SECOND_AT, CELLS_MID), bf16),
            pltpu.VMEM((LOCAL, CHANNELS, CELLS_MID), f32),
            pltpu.SemaphoreType.DMA((LOCAL,)),
            pltpu.SemaphoreType.DMA((5,)),
        ],
        compiler_params=pltpu.CompilerParams(vmem_limit_bytes=48 * MIB),
        cost_estimate=pl.CostEstimate(flops=3_200_000_000, bytes_accessed=14_000_000, transcendentals=700_000),
        name="forward",
    )(place, mine, other, x0, parents_fine, nb_mid, parents_mid, tiles)


def sign_smooth(v):
    return v * lax.rsqrt(v * v + SMOOTH)


def backward_kernel(
    place_ref, cohort0_ref, cohort1_ref, cohort2_ref, cohort3_ref, own_ref, obs_ref, x2_ref,
    parents_ref, nb_mid_ref, parents_mid_ref, w_hbm, tiles_mid_hbm, slope2_hbm, slope1_hbm, x_hbm, tiles_hbm,
    kept_ref, sent_ref,
    w_ref, tiles_mid_ref, slope2_ref, slope1_ref, x_ref, tiles_ref, g1_ref, sem,
):
    moves = ((w_hbm, w_ref), (slope2_hbm, slope2_ref), (tiles_mid_hbm, tiles_mid_ref), (slope1_hbm, slope1_ref), (x_hbm, x_ref), (tiles_hbm, tiles_ref))
    loads = [pltpu.make_async_copy(source, here, sem.at[i]) for i, (source, here) in enumerate(moves)]
    for load in loads:
        load.start()
    first = place_ref[0] == 0

    def put(quarter, at, lanes, value):
        for z in range(4):
            for y in range(4):
                row = (z * 4 + y) * 16
                low, high = value[row : row + 8], value[row + 8 : row + 16]
                kept_ref[quarter, y, z, :, at : at + lanes] = jnp.where(first, low, high).astype(bf16)
                sent_ref[quarter, y, z, :, at : at + lanes] = jnp.where(first, high, low).astype(bf16)

    own = own_ref[...]
    spread = jnp.zeros_like(own)
    for pair_ref in (cohort0_ref, cohort1_ref, cohort2_ref, cohort3_ref):
        for peer in range(2):
            theirs = pair_ref[peer]
            spread = spread + sign_smooth(own - theirs) + sign_smooth(own - pltpu.roll(theirs, CELLS_OUT, 1))
    skill = sign_smooth(own - obs_ref[...])
    slope = NORM * (skill / MEMBERS - spread / (MEMBERS * (MEMBERS - 1)))
    slope = jnp.concatenate([slope, jnp.zeros((128 - FIELD_ROWS, 128), f32)], 0).astype(bf16)
    put(3, 512, 128, dot_bt(x2_ref[...], slope))
    put(3, 640, 384, jnp.zeros((CHANNELS, 384), f32))
    pool = one_hot(parents_mid_ref[...], CELLS_OUT)
    wide = [dot(slope[:, m * CELLS_OUT : (m + 1) * CELLS_OUT], pool).astype(bf16) for m in range(LOCAL)]
    for load in loads[:4]:
        load.wait()
    head_t = w_ref[:, SECOND_AT:BACK_W]
    dh2 = [dot(head_t, wide[m]) * 0.25 for m in range(LOCAL)]
    g2 = [(dh2[m] * slope2_ref[m]).astype(bf16) for m in range(LOCAL)]
    both = jnp.concatenate(g2, 0)
    back = [dh2[m] + dot_at(w_ref[:, 0:CHANNELS], g2[m]) for m in range(LOCAL)]
    for q in range(1, SLOTS):
        spread_back = dot_bt(both, one_hot(nb_mid_ref[q : q + 1, :], CELLS_MID)).astype(bf16)
        weight = w_ref[:, q * CHANNELS : (q + 1) * CHANNELS]
        for m in range(LOCAL):
            back[m] = back[m] + dot_at(weight, spread_back[m * CHANNELS : (m + 1) * CHANNELS])
    unpool = one_hot(parents_ref[...], CELLS_MID)
    for m in range(LOCAL):
        dh1 = dot((back[m] * 0.25).astype(bf16), unpool)
        g1_ref[m] = (dh1 * slope1_ref[m].astype(f32)).astype(bf16)
    for load in loads[4:]:
        load.wait()
    for q in range(SLOTS):
        rows = slice(q * CHANNELS, (q + 1) * CHANNELS)
        grad = dot_bt(g2[0], tiles_mid_ref[0, rows]) + dot_bt(g2[1], tiles_mid_ref[1, rows])
        put((SLOTS + q) // 4, (SLOTS + q) % 4 * 256, 256, grad)
    put(0, 0, 256, dot_bt(g1_ref[0], x_ref[0]) + dot_bt(g1_ref[1], x_ref[1]))
    for j in range(1, SLOTS):
        grad = dot_bt(g1_ref[0], tiles_ref[0, j - 1]) + dot_bt(g1_ref[1], tiles_ref[1, j - 1])
        put(j // 4, j % 4 * 256, 256, grad)


def backward(place, cohort, own, obs, w, tiles_mid, slope2, x2, slope1, x0, tiles, parents_fine, nb_mid, parents_mid):
    return pl.pallas_call(
        backward_kernel,
        in_specs=[SMEM] + [VMEM] * 10 + [HBM] * 6,
        out_specs=[VMEM] * 2,
        out_shape=[jax.ShapeDtypeStruct((4, 4, 4, 8, QUARTER), bf16)] * 2,
        scratch_shapes=[
            pltpu.VMEM((CHANNELS, BACK_W), bf16),
            pltpu.VMEM((LOCAL, SECOND_AT, CELLS_MID), bf16),
            pltpu.VMEM((LOCAL, CHANNELS, CELLS_MID), f32),
            pltpu.VMEM((LOCAL, CHANNELS, CELLS_IN), bf16),
            pltpu.VMEM((LOCAL, CHANNELS, CELLS_IN), bf16),
            pltpu.VMEM(TILES, bf16),
            pltpu.VMEM((LOCAL, CHANNELS, CELLS_IN), bf16),
            pltpu.SemaphoreType.DMA((6,)),
        ],
        compiler_params=pltpu.CompilerParams(vmem_limit_bytes=50 * MIB),
        cost_estimate=pl.CostEstimate(flops=4_000_000_000, bytes_accessed=16_000_000, transcendentals=200_000),
        name="backward",
    )(place, *cohort, own, obs, x2, parents_fine, nb_mid, parents_mid, w, tiles_mid, slope2, slope1, x0, tiles)


def shift(v, axis, n, by):
    return lax.ppermute(v, axis, [(i, (i + by) % n) for i in range(n)])


def gather_weights(weight_first, weight_second, weight_head, x, tiles):
    rows = weight_first.shape[1]
    flat = jnp.concatenate(
        [
            weight_first.transpose(1, 0, 2).reshape(rows, SECOND_AT),
            weight_second.transpose(1, 0, 2).reshape(rows, SECOND_AT),
            weight_head.T,
            jnp.zeros((rows, WIDTH - HEAD_AT - FIELDS), bf16),
        ],
        1,
    )
    mine = lax.dynamic_slice_in_dim(flat, x * QUARTER, QUARTER, 1)
    column = spread([mine] + [shift(mine, "z_hi", 4, s) for s in (1, 2, 3)])
    plane = after(lax.all_to_all(column, ("x", "y"), 0, 0), tiles)
    return plane, shift(plane, "core", 2, 1)


def reduce_gradients(kept, sent, x):
    total = (kept.astype(f32) + shift(sent, "core", 2, 1).astype(f32)).astype(bf16)
    plane = lax.all_to_all(total.reshape(16, 4, 8, QUARTER), ("x", "y"), 0, 0)
    total = jnp.sum(plane.astype(f32), 0).astype(bf16)
    column = jnp.broadcast_to(total[:, None], (4, 2, 8, QUARTER)).reshape(8, 8, QUARTER)
    column = lax.all_to_all(column, ("z_hi", "z_lo"), 0, 0)
    total = jnp.sum(column.astype(f32), 0).astype(bf16)
    back = [total] + [shift(total, "x", 4, s) for s in (1, 2, 3)]
    ring = jnp.stack([back[i] for i in (3, 2, 1, 0, 3, 2, 1)])
    return lax.dynamic_slice_in_dim(ring, 3 - x, 4, 0).astype(f32).transpose(1, 0, 2).reshape(8, WIDTH)


def per_device(
    member_fields, weight_first, weight_second, weight_head,
    neighbours_fine, neighbours_mid, parents_fine, parents_mid, observations,
):
    core, x = lax.axis_index("core"), lax.axis_index("x")
    place = jnp.stack([core, lax.axis_index("z_hi")]).astype(jnp.int32)
    x0 = member_fields[0]
    parents_fine = parents_fine.reshape(1, CELLS_IN)
    parents_mid = parents_mid.reshape(1, CELLS_MID)
    truth = jnp.pad(observations[0], ((0, FIELD_ROWS - FIELDS), (0, 0)))
    truth = jnp.concatenate([truth] * LOCAL, 1)

    tiles = fine_tiles(x0.reshape(LOCAL * CHANNELS, CELLS_IN), neighbours_fine)
    mine, other = gather_weights(weight_first, weight_second, weight_head, x, tiles)
    x2, pred, slope1, w, tiles_mid, slope2 = forward(
        place, mine, other, x0, tiles, parents_fine, neighbours_mid, parents_mid
    )
    pair = jnp.stack([pred, shift(pred, "z_lo", 2, 1)])
    cohort = [pair] + [shift(pair, "x", 4, s) for s in (1, 2, 3)]
    kept, sent = backward(
        place, cohort, pred, truth, w, tiles_mid, slope2, x2, slope1, x0, tiles, parents_fine, neighbours_mid, parents_mid
    )
    rows = reduce_gradients(kept, sent, x)
    return (
        rows[:, :SECOND_AT].reshape(8, SLOTS, CHANNELS).transpose(1, 0, 2),
        rows[:, SECOND_AT:HEAD_AT].reshape(8, SLOTS, CHANNELS).transpose(1, 0, 2),
        rows[:, HEAD_AT : HEAD_AT + FIELDS].T,
    )


def solution(mesh):
    fine_mesh = Mesh(mesh.devices.reshape(2, 4, 4, 4, 2), ("z_lo", "x", "z_hi", "y", "core"))
    placed = (
        P(DP, MEM, None, None),
        P(None, DP, None),
        P(None, DP, None),
        P(None, DP),
        P(),
        P(),
        P(),
        P(),
        P(DP, None, None),
    )
    return jax.shard_map(
        per_device,
        mesh=fine_mesh,
        in_specs=placed,
        out_specs=(P(None, DP, None), P(None, DP, None), P(None, DP)),
        check_vma=False,
    )
```

```python
import math

import jax
import jax.numpy as jnp
from jax import lax
from jax.experimental import pallas as pl
from jax.experimental.pallas import tpu as pltpu
from jax.sharding import Mesh
from jax.sharding import PartitionSpec as P

DP = ("z_hi", "y", "core")
MEM = ("z_lo", "x")

MEMBERS = 16
CHANNELS = 256
SLOTS = 7
FIELDS = 69
FIELD_ROWS = 72
CELLS_OUT = 64
CELLS_MID = 256
CELLS_IN = 1024
SAMPLES = 32
LOCAL = 2
QUARTER = 1024
SMOOTH = 0.0001
NORM = MEMBERS / math.sqrt(SAMPLES * CELLS_OUT)
SECOND_AT = SLOTS * CHANNELS
HEAD_AT = 2 * SLOTS * CHANNELS
WIDTH = 4096
MIB = 1024 * 1024
TILES_MIB = 24
SAVED_ROWS = 8192
MID_AT, W_AT, SLOPE1_AT, SLOPE2_AT = 0, 3584, 5632, 7680

f32 = jnp.float32
bf16 = jnp.bfloat16


def dot(a, b):
    return lax.dot_general(a, b, (((1,), (0,)), ((), ())), preferred_element_type=f32)


def dot_bt(a, b):
    return lax.dot_general(a, b, (((1,), (1,)), ((), ())), preferred_element_type=f32)


def dot_at(a, b):
    return lax.dot_general(a, b, (((0,), (0,)), ((), ())), preferred_element_type=f32)


def one_hot(index_row, rows):
    shape = (rows, index_row.shape[1])
    return jnp.where(lax.broadcasted_iota(jnp.int32, shape, 0) == index_row, 1.0, 0.0).astype(bf16)


def tiles_kernel(x_ref, nb_ref, out_ref):
    row = nb_ref[pl.ds(pl.program_id(0) + 1, 1), :]
    tile = dot(x_ref[...], one_hot(row, CELLS_IN)).astype(bf16)
    for m in range(LOCAL):
        out_ref[m, 0] = tile[m * CHANNELS : (m + 1) * CHANNELS]


def fine_tiles(x0, nb):
    return pl.pallas_call(
        tiles_kernel,
        grid=(SLOTS - 1,),
        in_specs=[
            pl.BlockSpec((LOCAL * CHANNELS, CELLS_IN), lambda j: (0, 0)),
            pl.BlockSpec((SLOTS, CELLS_IN), lambda j: (0, 0)),
        ],
        out_specs=pl.BlockSpec((LOCAL, 1, CHANNELS, CELLS_IN), lambda j: (0, j, 0, 0)),
        out_shape=pltpu.HBM((LOCAL, SLOTS - 1, CHANNELS, CELLS_IN), bf16),
        compiler_params=pltpu.CompilerParams(vmem_limit_bytes=TILES_MIB * MIB),
        cost_estimate=pl.CostEstimate(flops=6_500_000_000, bytes_accessed=8_000_000, transcendentals=0),
        name="fine_tiles",
    )(x0, nb)


def forward_kernel(
    place_ref, mine_ref, other_ref, x_ref, parents_ref, nb_mid_ref, parents_mid_ref, tiles_hbm,
    x2_ref, pred_ref, saved_hbm,
    tiles_ref, w_ref, saved_ref, in_sem, out_sem,
):
    loads = [pltpu.make_async_copy(tiles_hbm.at[m], tiles_ref.at[m], in_sem.at[m]) for m in range(LOCAL)]
    for load in loads:
        load.start()
    first, z = place_ref[0] == 0, place_ref[1]
    for x in range(4):
        for y in range(4):
            for back in range(4):
                mine, other = mine_ref[x * 4 + y, back].astype(f32), other_ref[x * 4 + y, back].astype(f32)
                pair = jnp.concatenate([jnp.where(first, mine, other), jnp.where(first, other, mine)], 0)
                row = pl.multiple_of((lax.rem(z - back + 4, 4) * 4 + y) * 16, 16)
                w_ref[pl.ds(row, 16), x * QUARTER : (x + 1) * QUARTER] = pair.astype(bf16)
    saved_ref[W_AT + SECOND_AT : SLOPE1_AT, 128:256] = jnp.zeros((CHANNELS, 128), bf16)
    saved_ref[W_AT + SECOND_AT : SLOPE1_AT, 0:128] = w_ref[:, HEAD_AT : HEAD_AT + 128]
    for j in range(SLOTS):
        at = SECOND_AT + j * CHANNELS
        saved_ref[W_AT + j * CHANNELS : W_AT + (j + 1) * CHANNELS] = w_ref[:, at : at + CHANNELS]
    stores = []

    def save(begin, end):
        rows = slice(begin, end)
        stores.append(pltpu.make_async_copy(saved_ref.at[rows], saved_hbm.at[rows], out_sem.at[len(stores)]))
        stores[-1].start()

    save(W_AT, SLOPE1_AT)
    unpool = one_hot(parents_ref[...], CELLS_MID)
    x1 = []
    for m in range(LOCAL):
        loads[m].wait()
        pooled = jnp.zeros((CHANNELS, CELLS_MID), f32)
        for at in range(0, CELLS_IN, 512):
            cells = slice(at, at + 512)
            a1 = dot(w_ref[:, 0:CHANNELS], x_ref[m, :, cells])
            for j in range(1, SLOTS):
                a1 = a1 + dot(w_ref[:, j * CHANNELS : (j + 1) * CHANNELS], tiles_ref[m, j - 1, :, cells])
            gate = jax.nn.sigmoid(a1)
            slope1 = (gate * (1.0 + a1 * (1.0 - gate))).astype(bf16)
            for half in range(2):
                row = SLOPE1_AT + m * CELLS_IN + at + half * 256
                saved_ref[row : row + 256] = slope1[:, half * 256 : (half + 1) * 256]
            h1 = (x_ref[m, :, cells].astype(f32) + a1 * gate).astype(bf16)
            pooled = pooled + dot_bt(h1, unpool[:, cells])
        save(SLOPE1_AT + m * CELLS_IN, SLOPE1_AT + (m + 1) * CELLS_IN)
        x1.append((pooled * 0.25).astype(bf16))
        saved_ref[m * SECOND_AT : m * SECOND_AT + CHANNELS] = x1[m]
    both = jnp.concatenate(x1, 0)
    for j in range(1, SLOTS):
        tile = dot(both, one_hot(nb_mid_ref[j : j + 1, :], CELLS_MID)).astype(bf16)
        for m in range(LOCAL):
            row = m * SECOND_AT + j * CHANNELS
            saved_ref[row : row + CHANNELS] = tile[m * CHANNELS : (m + 1) * CHANNELS]
    save(MID_AT, W_AT)
    pool = one_hot(parents_mid_ref[...], CELLS_OUT)
    for m in range(LOCAL):
        a2 = dot(w_ref[:, SECOND_AT:HEAD_AT], saved_ref[m * SECOND_AT : (m + 1) * SECOND_AT])
        gate2 = jax.nn.sigmoid(a2)
        row = SLOPE2_AT + m * CHANNELS
        saved_ref[row : row + CHANNELS] = (gate2 * (1.0 + a2 * (1.0 - gate2))).astype(bf16)
        h2 = (x1[m].astype(f32) + a2 * gate2).astype(bf16)
        x2_ref[:, m * CELLS_OUT : (m + 1) * CELLS_OUT] = (dot_bt(h2, pool) * 0.25).astype(bf16)
    save(SLOPE2_AT, SAVED_ROWS)
    pred = dot_at(w_ref[:, HEAD_AT : HEAD_AT + 128], x2_ref[...])
    pred_ref[...] = pred[0:FIELD_ROWS]
    for store in stores:
        store.wait()


def spread_kernel(own_ref, back1_ref, back2_ref, back3_ref, out_ref):
    for block in range(16):
        for back, source in enumerate((own_ref, back1_ref, back2_ref, back3_ref)):
            out_ref[block, back] = source[...]


def spread(pieces):
    return pl.pallas_call(
        spread_kernel,
        in_specs=[pl.BlockSpec(memory_space=pltpu.VMEM)] * 4,
        out_specs=pl.BlockSpec(memory_space=pltpu.VMEM),
        out_shape=jax.ShapeDtypeStruct((16, 4, 8, QUARTER), bf16),
        compiler_params=pltpu.CompilerParams(vmem_limit_bytes=8 * MIB),
        name="spread",
    )(*pieces)


def after_kernel(value_ref, first_ref, out_ref):
    del value_ref, first_ref, out_ref


def after(value, first):
    return pl.pallas_call(
        after_kernel,
        in_specs=[pl.BlockSpec(memory_space=pl.ANY)] * 2,
        out_specs=pl.BlockSpec(memory_space=pl.ANY),
        out_shape=jax.ShapeDtypeStruct(value.shape, value.dtype),
        input_output_aliases={0: 0},
        compiler_params=pltpu.CompilerParams(vmem_limit_bytes=48 * MIB),
        name="after",
    )(value, first)


VMEM = pl.BlockSpec(memory_space=pltpu.VMEM)
HBM = pl.BlockSpec(memory_space=pltpu.HBM)
SMEM = pl.BlockSpec(memory_space=pltpu.SMEM)
TILES = (LOCAL, SLOTS - 1, CHANNELS, CELLS_IN)


def forward(place, mine, other, x0, tiles, parents_fine, nb_mid, parents_mid):
    return pl.pallas_call(
        forward_kernel,
        in_specs=[SMEM, VMEM, VMEM, VMEM, VMEM, VMEM, VMEM, HBM],
        out_specs=[VMEM, VMEM, HBM],
        out_shape=[
            jax.ShapeDtypeStruct((CHANNELS, LOCAL * CELLS_OUT), bf16),
            jax.ShapeDtypeStruct((FIELD_ROWS, LOCAL * CELLS_OUT), f32),
            pltpu.HBM((SAVED_ROWS, CELLS_MID), bf16),
        ],
        scratch_shapes=[
            pltpu.VMEM(TILES, bf16),
            pltpu.VMEM((CHANNELS, WIDTH), bf16),
            pltpu.VMEM((SAVED_ROWS, CELLS_MID), bf16),
            pltpu.SemaphoreType.DMA((LOCAL,)),
            pltpu.SemaphoreType.DMA((5,)),
        ],
        compiler_params=pltpu.CompilerParams(vmem_limit_bytes=48 * MIB),
        cost_estimate=pl.CostEstimate(flops=3_200_000_000, bytes_accessed=14_000_000, transcendentals=700_000),
        name="forward",
    )(place, mine, other, x0, parents_fine, nb_mid, parents_mid, tiles)


def sign_smooth(v):
    return v * lax.rsqrt(v * v + SMOOTH)


def backward_kernel(
    place_ref, cohort0_ref, cohort1_ref, cohort2_ref, cohort3_ref, own_ref, obs_ref, x2_ref,
    parents_ref, nb_mid_ref, parents_mid_ref, saved_hbm, x_hbm, tiles_hbm,
    kept_ref, sent_ref,
    saved_ref, x_ref, tiles_ref, g1_ref, sem,
):
    moves = ((saved_hbm, saved_ref), (x_hbm, x_ref), (tiles_hbm, tiles_ref))
    loads = [pltpu.make_async_copy(source, here, sem.at[i]) for i, (source, here) in enumerate(moves)]
    for load in loads:
        load.start()
    first = place_ref[0] == 0

    def put(quarter, at, lanes, value):
        for z in range(4):
            for y in range(4):
                row = (z * 4 + y) * 16
                low, high = value[row : row + 8], value[row + 8 : row + 16]
                kept_ref[quarter, y, z, :, at : at + lanes] = jnp.where(first, low, high).astype(bf16)
                sent_ref[quarter, y, z, :, at : at + lanes] = jnp.where(first, high, low).astype(bf16)

    own = own_ref[...]
    spread = jnp.zeros_like(own)
    for pair_ref in (cohort0_ref, cohort1_ref, cohort2_ref, cohort3_ref):
        for peer in range(2):
            theirs = pair_ref[peer]
            spread = spread + sign_smooth(own - theirs) + sign_smooth(own - pltpu.roll(theirs, CELLS_OUT, 1))
    skill = sign_smooth(own - obs_ref[...])
    slope = NORM * (skill / MEMBERS - spread / (MEMBERS * (MEMBERS - 1)))
    slope = jnp.concatenate([slope, jnp.zeros((128 - FIELD_ROWS, 128), f32)], 0).astype(bf16)
    put(3, 512, 128, dot_bt(x2_ref[...], slope))
    put(3, 640, 384, jnp.zeros((CHANNELS, 384), f32))
    pool = one_hot(parents_mid_ref[...], CELLS_OUT)
    wide = [dot(slope[:, m * CELLS_OUT : (m + 1) * CELLS_OUT], pool).astype(bf16) for m in range(LOCAL)]
    loads[0].wait()
    head_t = saved_ref[W_AT + SECOND_AT : SLOPE1_AT, 0:128]
    dh2 = [dot(head_t, wide[m]) * 0.25 for m in range(LOCAL)]
    slope2 = saved_ref[SLOPE2_AT:SAVED_ROWS].astype(f32)
    g2 = [(dh2[m] * slope2[m * CHANNELS : (m + 1) * CHANNELS]).astype(bf16) for m in range(LOCAL)]
    both = jnp.concatenate(g2, 0)
    back = [dh2[m] + dot_at(saved_ref[W_AT : W_AT + CHANNELS], g2[m]) for m in range(LOCAL)]
    for q in range(1, SLOTS):
        spread_back = dot_bt(both, one_hot(nb_mid_ref[q : q + 1, :], CELLS_MID)).astype(bf16)
        weight = saved_ref[W_AT + q * CHANNELS : W_AT + (q + 1) * CHANNELS]
        for m in range(LOCAL):
            back[m] = back[m] + dot_at(weight, spread_back[m * CHANNELS : (m + 1) * CHANNELS])
    unpool = one_hot(parents_ref[...], CELLS_MID)
    for m in range(LOCAL):
        dh1 = dot((back[m] * 0.25).astype(bf16), unpool)
        for at in range(0, CELLS_IN, 256):
            slope1 = saved_ref[SLOPE1_AT + m * CELLS_IN + at : SLOPE1_AT + m * CELLS_IN + at + 256].astype(f32)
            g1_ref[m, :, at : at + 256] = (dh1[:, at : at + 256] * slope1).astype(bf16)
    for load in loads[1:]:
        load.wait()
    for q in range(SLOTS):
        row0, row1 = q * CHANNELS, SECOND_AT + q * CHANNELS
        grad = dot_bt(g2[0], saved_ref[row0 : row0 + CHANNELS]) + dot_bt(g2[1], saved_ref[row1 : row1 + CHANNELS])
        put((SLOTS + q) // 4, (SLOTS + q) % 4 * 256, 256, grad)
    put(0, 0, 256, dot_bt(g1_ref[0], x_ref[0]) + dot_bt(g1_ref[1], x_ref[1]))
    for j in range(1, SLOTS):
        grad = dot_bt(g1_ref[0], tiles_ref[0, j - 1]) + dot_bt(g1_ref[1], tiles_ref[1, j - 1])
        put(j // 4, j % 4 * 256, 256, grad)


def backward(place, cohort, own, obs, x2, saved, x0, tiles, parents_fine, nb_mid, parents_mid):
    return pl.pallas_call(
        backward_kernel,
        in_specs=[SMEM] + [VMEM] * 10 + [HBM] * 3,
        out_specs=[VMEM] * 2,
        out_shape=[jax.ShapeDtypeStruct((4, 4, 4, 8, QUARTER), bf16)] * 2,
        scratch_shapes=[
            pltpu.VMEM((SAVED_ROWS, CELLS_MID), bf16),
            pltpu.VMEM((LOCAL, CHANNELS, CELLS_IN), bf16),
            pltpu.VMEM(TILES, bf16),
            pltpu.VMEM((LOCAL, CHANNELS, CELLS_IN), bf16),
            pltpu.SemaphoreType.DMA((3,)),
        ],
        compiler_params=pltpu.CompilerParams(vmem_limit_bytes=50 * MIB),
        cost_estimate=pl.CostEstimate(flops=4_000_000_000, bytes_accessed=16_000_000, transcendentals=200_000),
        name="backward",
    )(place, *cohort, own, obs, x2, parents_fine, nb_mid, parents_mid, saved, x0, tiles)


def shift(v, axis, n, by):
    return lax.ppermute(v, axis, [(i, (i + by) % n) for i in range(n)])


def gather_weights(weight_first, weight_second, weight_head, x, tiles):
    rows = weight_first.shape[1]
    flat = jnp.concatenate(
        [
            weight_first.transpose(1, 0, 2).reshape(rows, SECOND_AT),
            weight_second.transpose(1, 0, 2).reshape(rows, SECOND_AT),
            weight_head.T,
            jnp.zeros((rows, WIDTH - HEAD_AT - FIELDS), bf16),
        ],
        1,
    )
    mine = lax.dynamic_slice_in_dim(flat, x * QUARTER, QUARTER, 1)
    column = spread([mine] + [shift(mine, "z_hi", 4, s) for s in (1, 2, 3)])
    plane = after(lax.all_to_all(column, ("x", "y"), 0, 0), tiles)
    return plane, shift(plane, "core", 2, 1)


def reduce_gradients(kept, sent, x):
    total = (kept.astype(f32) + shift(sent, "core", 2, 1).astype(f32)).astype(bf16)
    plane = lax.all_to_all(total.reshape(16, 4, 8, QUARTER), ("x", "y"), 0, 0)
    total = jnp.sum(plane.astype(f32), 0).astype(bf16)
    column = jnp.broadcast_to(total[:, None], (4, 2, 8, QUARTER)).reshape(8, 8, QUARTER)
    column = lax.all_to_all(column, ("z_hi", "z_lo"), 0, 0)
    total = jnp.sum(column.astype(f32), 0).astype(bf16)
    return finish(x.astype(jnp.int32).reshape(1), [total] + [shift(total, "x", 4, s) for s in (1, 2, 3)])


def finish_kernel(x_ref, own_ref, back1_ref, back2_ref, back3_ref, first_ref, second_ref, head_ref, slots_ref):
    for back, source in enumerate((own_ref, back1_ref, back2_ref, back3_ref)):
        at = lax.rem(x_ref[0] - back + 4, 4) * 4
        for slot in range(4):
            slots_ref[at + slot] = source[:, slot * CHANNELS : (slot + 1) * CHANNELS].astype(f32)
    first_ref[...] = slots_ref[0:SLOTS]
    second_ref[...] = slots_ref[SLOTS : 2 * SLOTS]
    head_ref[...] = slots_ref[2 * SLOTS, :, 0:FIELDS]


def finish(x, quarters):
    return pl.pallas_call(
        finish_kernel,
        in_specs=[SMEM] + [VMEM] * 4,
        out_specs=[VMEM] * 3,
        out_shape=[
            jax.ShapeDtypeStruct((SLOTS, 8, CHANNELS), f32),
            jax.ShapeDtypeStruct((SLOTS, 8, CHANNELS), f32),
            jax.ShapeDtypeStruct((8, FIELDS), f32),
        ],
        scratch_shapes=[pltpu.VMEM((16, 8, CHANNELS), f32)],
        compiler_params=pltpu.CompilerParams(vmem_limit_bytes=16 * MIB),
        name="finish",
    )(x, *quarters)


def per_device(
    member_fields, weight_first, weight_second, weight_head,
    neighbours_fine, neighbours_mid, parents_fine, parents_mid, observations,
):
    core, x = lax.axis_index("core"), lax.axis_index("x")
    place = jnp.stack([core, lax.axis_index("z_hi")]).astype(jnp.int32)
    x0 = member_fields[0]
    parents_fine = parents_fine.reshape(1, CELLS_IN)
    parents_mid = parents_mid.reshape(1, CELLS_MID)
    truth = jnp.pad(observations[0], ((0, FIELD_ROWS - FIELDS), (0, 0)))
    truth = jnp.concatenate([truth] * LOCAL, 1)

    tiles = fine_tiles(x0.reshape(LOCAL * CHANNELS, CELLS_IN), neighbours_fine)
    mine, other = gather_weights(weight_first, weight_second, weight_head, x, tiles)
    x2, pred, saved = forward(
        place, mine, other, x0, tiles, parents_fine, neighbours_mid, parents_mid
    )
    pair = jnp.stack([pred, shift(pred, "z_lo", 2, 1)])
    cohort = [pair] + [shift(pair, "x", 4, s) for s in (1, 2, 3)]
    kept, sent = backward(place, cohort, pred, truth, x2, saved, x0, tiles, parents_fine, neighbours_mid, parents_mid)
    grad_first, grad_second, grad_head = reduce_gradients(kept, sent, x)
    return grad_first, grad_second, grad_head.T


def solution(mesh):
    fine_mesh = Mesh(mesh.devices.reshape(2, 4, 4, 4, 2), ("z_lo", "x", "z_hi", "y", "core"))
    placed = (
        P(DP, MEM, None, None),
        P(None, DP, None),
        P(None, DP, None),
        P(None, DP),
        P(),
        P(),
        P(),
        P(),
        P(DP, None, None),
    )
    return jax.shard_map(
        per_device,
        mesh=fine_mesh,
        in_specs=placed,
        out_specs=(P(None, DP, None), P(None, DP, None), P(None, DP)),
        check_vma=False,
    )
```

```python
import math

import jax
import jax.numpy as jnp
from jax import lax
from jax.experimental import pallas as pl
from jax.experimental.pallas import tpu as pltpu
from jax.sharding import Mesh
from jax.sharding import PartitionSpec as P

DP = ("z_hi", "y", "core")
MEM = ("z_lo", "x")

MEMBERS = 16
CHANNELS = 256
SLOTS = 7
FIELDS = 69
FIELD_ROWS = 72
CELLS_OUT = 64
CELLS_MID = 256
CELLS_IN = 1024
SAMPLES = 32
LOCAL = 2
QUARTER = 1024
SMOOTH = 0.0001
NORM = MEMBERS / math.sqrt(SAMPLES * CELLS_OUT)
SECOND_AT = SLOTS * CHANNELS
HEAD_AT = 2 * SLOTS * CHANNELS
PART = 896
SHARE = 32
WIDTH = HEAD_AT + 128
MIB = 1024 * 1024
TILES_MIB = 24
SAVED_ROWS = 8192
MID_AT, SLOPE1_AT, W_AT, SLOPE2_AT = 0, 3584, 5632, 7680

f32 = jnp.float32
bf16 = jnp.bfloat16


def dot(a, b):
    return lax.dot_general(a, b, (((1,), (0,)), ((), ())), preferred_element_type=f32)


def dot_bt(a, b):
    return lax.dot_general(a, b, (((1,), (1,)), ((), ())), preferred_element_type=f32)


def dot_at(a, b):
    return lax.dot_general(a, b, (((0,), (0,)), ((), ())), preferred_element_type=f32)


def one_hot(index_row, rows):
    shape = (rows, index_row.shape[1])
    return jnp.where(lax.broadcasted_iota(jnp.int32, shape, 0) == index_row, 1.0, 0.0).astype(bf16)


def tiles_kernel(x_ref, nb_ref, out_ref):
    row = nb_ref[pl.ds(pl.program_id(0) + 1, 1), :]
    tile = dot(x_ref[...], one_hot(row, CELLS_IN)).astype(bf16)
    for m in range(LOCAL):
        out_ref[m, 0] = tile[m * CHANNELS : (m + 1) * CHANNELS]


def fine_tiles(x0, nb):
    return pl.pallas_call(
        tiles_kernel,
        grid=(SLOTS - 1,),
        in_specs=[
            pl.BlockSpec((LOCAL * CHANNELS, CELLS_IN), lambda j: (0, 0)),
            pl.BlockSpec((SLOTS, CELLS_IN), lambda j: (0, 0)),
        ],
        out_specs=pl.BlockSpec((LOCAL, 1, CHANNELS, CELLS_IN), lambda j: (0, j, 0, 0)),
        out_shape=pltpu.HBM((LOCAL, SLOTS - 1, CHANNELS, CELLS_IN), bf16),
        compiler_params=pltpu.CompilerParams(vmem_limit_bytes=TILES_MIB * MIB),
        cost_estimate=pl.CostEstimate(flops=6_500_000_000, bytes_accessed=8_000_000, transcendentals=0),
        name="fine_tiles",
    )(x0, nb)


def forward_kernel(
    place_ref, mine_ref, other_ref, x_ref, parents_ref, nb_mid_ref, parents_mid_ref, tiles_hbm,
    x2_ref, pred_ref, saved_hbm,
    tiles_ref, w_ref, saved_ref, select_ref, in_sem, out_sem,
):
    loads = [pltpu.make_async_copy(tiles_hbm.at[m], tiles_ref.at[m], in_sem.at[m]) for m in range(LOCAL)]
    for load in loads:
        load.start()
    first, z = place_ref[0] == 0, place_ref[1]
    group = lane_group(16)

    def both_rows(block, lanes):
        mine, other = mine_ref[block, :, lanes].astype(f32), other_ref[block, :, lanes].astype(f32)
        return jnp.concatenate([jnp.where(first, mine, other), jnp.where(first, other, mine)], 0)

    for y in range(4):
        rows = [pl.ds(pl.multiple_of((lax.rem(z - back + 4, 4) * 4 + y) * 16, 16), 16) for back in range(4)]
        for x in range(4):
            for back in range(4):
                part = both_rows(x * 4 + y, slice(back * PART, (back + 1) * PART))
                w_ref[rows[back], x * PART : (x + 1) * PART] = part.astype(bf16)
        shares = [both_rows(x * 4 + y, slice(HEAD_AT, WIDTH)) for x in range(4)]
        for back in range(4):
            head = jnp.zeros((16, 128), f32)
            for x in range(4):
                head = jnp.where(group == x, pltpu.roll(shares[x], (x - back) % 4 * SHARE, 1), head)
            w_ref[rows[back], HEAD_AT:WIDTH] = head.astype(bf16)
    saved_ref[W_AT + SECOND_AT : SLOPE2_AT, 128:256] = jnp.zeros((CHANNELS, 128), bf16)
    saved_ref[W_AT + SECOND_AT : SLOPE2_AT, 0:128] = w_ref[:, HEAD_AT : HEAD_AT + 128]
    for j in range(SLOTS):
        at = SECOND_AT + j * CHANNELS
        saved_ref[W_AT + j * CHANNELS : W_AT + (j + 1) * CHANNELS] = w_ref[:, at : at + CHANNELS]
    stores = []

    def save(begin, end):
        rows = slice(begin, end)
        stores.append(pltpu.make_async_copy(saved_ref.at[rows], saved_hbm.at[rows], out_sem.at[len(stores)]))
        stores[-1].start()

    save(W_AT, SLOPE2_AT)
    unpool = one_hot(parents_ref[...], CELLS_MID)
    for j in range(1, SLOTS):
        select_ref[j - 1] = one_hot(nb_mid_ref[j : j + 1, :], CELLS_MID)
    x1 = []
    for m in range(LOCAL):
        loads[m].wait()
        pooled = jnp.zeros((CHANNELS, CELLS_MID), f32)
        for at in range(0, CELLS_IN, 512):
            cells = slice(at, at + 512)
            a1 = dot(w_ref[:, 0:CHANNELS], x_ref[m, :, cells])
            for j in range(1, SLOTS):
                a1 = a1 + dot(w_ref[:, j * CHANNELS : (j + 1) * CHANNELS], tiles_ref[m, j - 1, :, cells])
            gate = jax.nn.sigmoid(a1)
            slope1 = (gate * (1.0 + a1 * (1.0 - gate))).astype(bf16)
            for half in range(2):
                row = SLOPE1_AT + m * CELLS_IN + at + half * 256
                saved_ref[row : row + 256] = slope1[:, half * 256 : (half + 1) * 256]
            h1 = (x_ref[m, :, cells].astype(f32) + a1 * gate).astype(bf16)
            pooled = pooled + dot_bt(h1, unpool[:, cells])
        save(SLOPE1_AT + m * CELLS_IN, SLOPE1_AT + (m + 1) * CELLS_IN)
        x1.append((pooled * 0.25).astype(bf16))
        saved_ref[m * SECOND_AT : m * SECOND_AT + CHANNELS] = x1[m]
    both = jnp.concatenate(x1, 0)
    for j in range(1, SLOTS):
        tile = dot(both, select_ref[j - 1]).astype(bf16)
        for m in range(LOCAL):
            row = m * SECOND_AT + j * CHANNELS
            saved_ref[row : row + CHANNELS] = tile[m * CHANNELS : (m + 1) * CHANNELS]
    save(MID_AT, SLOPE1_AT)
    pool = one_hot(parents_mid_ref[...], CELLS_OUT)
    for m in range(LOCAL):
        a2 = dot(w_ref[:, SECOND_AT:HEAD_AT], saved_ref[m * SECOND_AT : (m + 1) * SECOND_AT])
        gate2 = jax.nn.sigmoid(a2)
        row = SLOPE2_AT + m * CHANNELS
        saved_ref[row : row + CHANNELS] = (gate2 * (1.0 + a2 * (1.0 - gate2))).astype(bf16)
        h2 = (x1[m].astype(f32) + a2 * gate2).astype(bf16)
        x2_ref[:, m * CELLS_OUT : (m + 1) * CELLS_OUT] = (dot_bt(h2, pool) * 0.25).astype(bf16)
    save(SLOPE2_AT, SAVED_ROWS)
    pred = dot_at(w_ref[:, HEAD_AT : HEAD_AT + 128], x2_ref[...])
    pred_ref[...] = pred[0:FIELD_ROWS]
    for store in stores:
        store.wait()


def lane_group(rows):
    return lax.div(lax.broadcasted_iota(jnp.int32, (rows, 128), 1), SHARE)


def spread_kernel(own_ref, back1_ref, back2_ref, back3_ref, out_ref):
    sources = (own_ref, back1_ref, back2_ref, back3_ref)
    head = own_ref[:, PART:QUARTER].astype(f32)
    for back in range(1, 4):
        head = head + pltpu.roll(sources[back][:, PART:QUARTER].astype(f32), back * SHARE, 1)
    head = head.astype(bf16)
    for block in range(16):
        for back in range(4):
            out_ref[block, :, back * PART : (back + 1) * PART] = sources[back][:, 0:PART]
        out_ref[block, :, HEAD_AT:WIDTH] = head


def spread(pieces):
    return pl.pallas_call(
        spread_kernel,
        in_specs=[pl.BlockSpec(memory_space=pltpu.VMEM)] * 4,
        out_specs=pl.BlockSpec(memory_space=pltpu.VMEM),
        out_shape=jax.ShapeDtypeStruct((16, 8, WIDTH), bf16),
        compiler_params=pltpu.CompilerParams(vmem_limit_bytes=8 * MIB),
        name="spread",
    )(*pieces)


def after_kernel(value_ref, first_ref, out_ref):
    del value_ref, first_ref, out_ref


def after(value, first):
    return pl.pallas_call(
        after_kernel,
        in_specs=[pl.BlockSpec(memory_space=pl.ANY)] * 2,
        out_specs=pl.BlockSpec(memory_space=pl.ANY),
        out_shape=jax.ShapeDtypeStruct(value.shape, value.dtype),
        input_output_aliases={0: 0},
        compiler_params=pltpu.CompilerParams(vmem_limit_bytes=48 * MIB),
        name="after",
    )(value, first)


VMEM = pl.BlockSpec(memory_space=pltpu.VMEM)
HBM = pl.BlockSpec(memory_space=pltpu.HBM)
SMEM = pl.BlockSpec(memory_space=pltpu.SMEM)
TILES = (LOCAL, SLOTS - 1, CHANNELS, CELLS_IN)


def forward(place, mine, other, x0, tiles, parents_fine, nb_mid, parents_mid):
    return pl.pallas_call(
        forward_kernel,
        in_specs=[SMEM, VMEM, VMEM, VMEM, VMEM, VMEM, VMEM, HBM],
        out_specs=[VMEM, VMEM, HBM],
        out_shape=[
            jax.ShapeDtypeStruct((CHANNELS, LOCAL * CELLS_OUT), bf16),
            jax.ShapeDtypeStruct((FIELD_ROWS, LOCAL * CELLS_OUT), f32),
            pltpu.HBM((SAVED_ROWS, CELLS_MID), bf16),
        ],
        scratch_shapes=[
            pltpu.VMEM(TILES, bf16),
            pltpu.VMEM((CHANNELS, WIDTH), bf16),
            pltpu.VMEM((SAVED_ROWS, CELLS_MID), bf16),
            pltpu.VMEM((SLOTS - 1, CELLS_MID, CELLS_MID), bf16),
            pltpu.SemaphoreType.DMA((LOCAL,)),
            pltpu.SemaphoreType.DMA((5,)),
        ],
        compiler_params=pltpu.CompilerParams(vmem_limit_bytes=48 * MIB),
        cost_estimate=pl.CostEstimate(flops=3_200_000_000, bytes_accessed=14_000_000, transcendentals=700_000),
        name="forward",
    )(place, mine, other, x0, parents_fine, nb_mid, parents_mid, tiles)


def sign_smooth(v):
    return v * lax.rsqrt(v * v + SMOOTH)


def backward_kernel(
    place_ref, cohort0_ref, cohort1_ref, cohort2_ref, cohort3_ref, own_ref, obs_ref, x2_ref,
    parents_ref, nb_mid_ref, parents_mid_ref, saved_hbm, x_hbm, tiles_hbm,
    kept_ref, sent_ref,
    saved_ref, x_ref, tiles_ref, g1_ref, select_ref, unpool_ref, sem,
):
    early, late = pl.ds(W_AT, SAVED_ROWS - W_AT), pl.ds(0, W_AT)
    moves = (
        (saved_hbm.at[early], saved_ref.at[early]), (saved_hbm.at[late], saved_ref.at[late]), (x_hbm, x_ref), (tiles_hbm, tiles_ref)
    )
    loads = [pltpu.make_async_copy(source, here, sem.at[i]) for i, (source, here) in enumerate(moves)]
    for load in loads:
        load.start()
    first = place_ref[0] == 0

    def put_rows(quarter, y, lanes, value0, value1):
        kept_ref[quarter, y, :, lanes] = jnp.where(first, value0, value1).astype(bf16)
        sent_ref[quarter, y, :, lanes] = jnp.where(first, value1, value0).astype(bf16)

    def put(piece, value):
        at = piece * 256
        cuts = [0, 128, 256] if at // PART != (at + 128) // PART else [0, 256]
        for begin, end in zip(cuts[:-1], cuts[1:]):
            quarter, offset = (at + begin) // PART, (at + begin) % PART
            for z in range(4):
                lanes = slice(z * PART + offset, z * PART + offset + end - begin)
                for y in range(4):
                    row = (z * 4 + y) * 16
                    put_rows(quarter, y, lanes, value[row : row + 8, begin:end], value[row + 8 : row + 16, begin:end])

    def put_head(value):
        group = lane_group(16)
        for quarter in range(4):
            for y in range(4):
                packed = jnp.zeros((16, 128), f32)
                for z in range(4):
                    row = (z * 4 + y) * 16
                    packed = jnp.where(group == z, pltpu.roll(value[row : row + 16], (z - quarter) % 4 * SHARE, 1), packed)
                put_rows(quarter, y, slice(HEAD_AT, WIDTH), packed[0:8], packed[8:16])

    own = own_ref[...]
    spread = jnp.zeros_like(own)
    for pair_ref in (cohort0_ref, cohort1_ref, cohort2_ref, cohort3_ref):
        for peer in range(2):
            theirs = pair_ref[peer]
            spread = spread + sign_smooth(own - theirs) + sign_smooth(own - pltpu.roll(theirs, CELLS_OUT, 1))
    skill = sign_smooth(own - obs_ref[...])
    slope = NORM * (skill / MEMBERS - spread / (MEMBERS * (MEMBERS - 1)))
    slope = jnp.concatenate([slope, jnp.zeros((128 - FIELD_ROWS, 128), f32)], 0).astype(bf16)
    put_head(dot_bt(x2_ref[...], slope))
    pool = one_hot(parents_mid_ref[...], CELLS_OUT)
    wide = [dot(slope[:, m * CELLS_OUT : (m + 1) * CELLS_OUT], pool).astype(bf16) for m in range(LOCAL)]
    for j in range(1, SLOTS):
        select_ref[j - 1] = one_hot(nb_mid_ref[j : j + 1, :], CELLS_MID)
    unpool_ref[...] = one_hot(parents_ref[...], CELLS_MID)
    loads[0].wait()
    head_t = saved_ref[W_AT + SECOND_AT : SLOPE2_AT, 0:128]
    dh2 = [dot(head_t, wide[m]) * 0.25 for m in range(LOCAL)]
    slope2 = saved_ref[SLOPE2_AT:SAVED_ROWS].astype(f32)
    g2 = [(dh2[m] * slope2[m * CHANNELS : (m + 1) * CHANNELS]).astype(bf16) for m in range(LOCAL)]
    both = jnp.concatenate(g2, 0)
    back = [dh2[m] + dot_at(saved_ref[W_AT : W_AT + CHANNELS], g2[m]) for m in range(LOCAL)]
    for q in range(1, SLOTS):
        spread_back = dot_bt(both, select_ref[q - 1]).astype(bf16)
        weight = saved_ref[W_AT + q * CHANNELS : W_AT + (q + 1) * CHANNELS]
        for m in range(LOCAL):
            back[m] = back[m] + dot_at(weight, spread_back[m * CHANNELS : (m + 1) * CHANNELS])
    loads[1].wait()
    for m in range(LOCAL):
        dh1 = dot((back[m] * 0.25).astype(bf16), unpool_ref[...])
        for at in range(0, CELLS_IN, 256):
            slope1 = saved_ref[SLOPE1_AT + m * CELLS_IN + at : SLOPE1_AT + m * CELLS_IN + at + 256].astype(f32)
            g1_ref[m, :, at : at + 256] = (dh1[:, at : at + 256] * slope1).astype(bf16)
    for load in loads[2:]:
        load.wait()
    for q in range(SLOTS):
        row0, row1 = q * CHANNELS, SECOND_AT + q * CHANNELS
        grad = dot_bt(g2[0], saved_ref[row0 : row0 + CHANNELS]) + dot_bt(g2[1], saved_ref[row1 : row1 + CHANNELS])
        put(SLOTS + q, grad)
    put(0, dot_bt(g1_ref[0], x_ref[0]) + dot_bt(g1_ref[1], x_ref[1]))
    for j in range(1, SLOTS):
        grad = dot_bt(g1_ref[0], tiles_ref[0, j - 1]) + dot_bt(g1_ref[1], tiles_ref[1, j - 1])
        put(j, grad)


def backward(place, cohort, own, obs, x2, saved, x0, tiles, parents_fine, nb_mid, parents_mid):
    return pl.pallas_call(
        backward_kernel,
        in_specs=[SMEM] + [VMEM] * 10 + [HBM] * 3,
        out_specs=[VMEM] * 2,
        out_shape=[jax.ShapeDtypeStruct((4, 4, 8, WIDTH), bf16)] * 2,
        scratch_shapes=[
            pltpu.VMEM((SAVED_ROWS, CELLS_MID), bf16),
            pltpu.VMEM((LOCAL, CHANNELS, CELLS_IN), bf16),
            pltpu.VMEM(TILES, bf16),
            pltpu.VMEM((LOCAL, CHANNELS, CELLS_IN), bf16),
            pltpu.VMEM((SLOTS - 1, CELLS_MID, CELLS_MID), bf16),
            pltpu.VMEM((CELLS_MID, CELLS_IN), bf16),
            pltpu.SemaphoreType.DMA((4,)),
        ],
        compiler_params=pltpu.CompilerParams(vmem_limit_bytes=50 * MIB),
        cost_estimate=pl.CostEstimate(flops=4_000_000_000, bytes_accessed=16_000_000, transcendentals=200_000),
        name="backward",
    )(place, *cohort, own, obs, x2, parents_fine, nb_mid, parents_mid, saved, x0, tiles)


def shift(v, axis, n, by):
    return lax.ppermute(v, axis, [(i, (i + by) % n) for i in range(n)])


def gather_weights(weight_first, weight_second, weight_head, x, tiles):
    rows = weight_first.shape[1]
    flat = jnp.concatenate(
        [
            weight_first.transpose(1, 0, 2).reshape(rows, SECOND_AT),
            weight_second.transpose(1, 0, 2).reshape(rows, SECOND_AT),
            weight_head.T,
            jnp.zeros((rows, WIDTH - HEAD_AT - FIELDS), bf16),
        ],
        1,
    )
    mine = jnp.concatenate(
        [
            lax.dynamic_slice_in_dim(flat, x * PART, PART, 1),
            lax.dynamic_slice_in_dim(flat, HEAD_AT + x * SHARE, SHARE, 1),
            jnp.zeros((rows, QUARTER - PART - SHARE), bf16),
        ],
        1,
    )
    column = spread([mine] + [shift(mine, "z_hi", 4, s) for s in (1, 2, 3)])
    plane = after(lax.all_to_all(column, ("x", "y"), 0, 0), tiles)
    return plane, shift(plane, "core", 2, 1)


def fold_kernel(plane_ref, out_ref):
    total = plane_ref[0].astype(f32)
    for block in range(1, 16):
        total = total + plane_ref[block].astype(f32)
    head, group = total[:, HEAD_AT:WIDTH], lane_group(8)
    for z in range(4):
        share = jnp.where(group == 0, pltpu.roll(head, -z % 4 * SHARE, 1), 0.0).astype(bf16)
        for low in range(2):
            out_ref[z * 2 + low, :, 0:PART] = total[:, z * PART : (z + 1) * PART].astype(bf16)
            out_ref[z * 2 + low, :, PART:QUARTER] = share


def fold(plane):
    return pl.pallas_call(
        fold_kernel,
        in_specs=[VMEM],
        out_specs=VMEM,
        out_shape=jax.ShapeDtypeStruct((8, 8, QUARTER), bf16),
        compiler_params=pltpu.CompilerParams(vmem_limit_bytes=8 * MIB),
        name="fold",
    )(plane)


def reduce_gradients(kept, sent, x):
    total = (kept.astype(f32) + shift(sent, "core", 2, 1).astype(f32)).astype(bf16)
    column = fold(lax.all_to_all(total.reshape(16, 8, WIDTH), ("x", "y"), 0, 0))
    column = lax.all_to_all(column, ("z_hi", "z_lo"), 0, 0)
    total = jnp.sum(column.astype(f32), 0).astype(bf16)
    return finish(x.astype(jnp.int32).reshape(1), [total] + [shift(total, "x", 4, s) for s in (1, 2, 3)])


def finish_kernel(x_ref, own_ref, back1_ref, back2_ref, back3_ref, first_ref, second_ref, head_ref, flat_ref, heads_ref):
    for back, source in enumerate((own_ref, back1_ref, back2_ref, back3_ref)):
        quarter = lax.rem(x_ref[0] - back + 4, 4)
        flat_ref[:, pl.ds(pl.multiple_of(quarter * PART, 128), PART)] = source[:, 0:PART].astype(f32)
        heads_ref[quarter] = source[:, PART:QUARTER].astype(f32)
    for j in range(SLOTS):
        first_ref[j] = flat_ref[:, j * CHANNELS : (j + 1) * CHANNELS]
        second_ref[j] = flat_ref[:, SECOND_AT + j * CHANNELS : SECOND_AT + (j + 1) * CHANNELS]
    head = heads_ref[0]
    for x in range(1, 4):
        head = head + pltpu.roll(heads_ref[x], x * SHARE, 1)
    head_ref[...] = head[:, 0:FIELDS]


def finish(x, quarters):
    return pl.pallas_call(
        finish_kernel,
        in_specs=[SMEM] + [VMEM] * 4,
        out_specs=[VMEM] * 3,
        out_shape=[
            jax.ShapeDtypeStruct((SLOTS, 8, CHANNELS), f32),
            jax.ShapeDtypeStruct((SLOTS, 8, CHANNELS), f32),
            jax.ShapeDtypeStruct((8, FIELDS), f32),
        ],
        scratch_shapes=[pltpu.VMEM((8, HEAD_AT), f32), pltpu.VMEM((4, 8, 128), f32)],
        compiler_params=pltpu.CompilerParams(vmem_limit_bytes=16 * MIB),
        name="finish",
    )(x, *quarters)


def per_device(
    member_fields, weight_first, weight_second, weight_head,
    neighbours_fine, neighbours_mid, parents_fine, parents_mid, observations,
):
    core, x = lax.axis_index("core"), lax.axis_index("x")
    place = jnp.stack([core, lax.axis_index("z_hi")]).astype(jnp.int32)
    x0 = member_fields[0]
    parents_fine = parents_fine.reshape(1, CELLS_IN)
    parents_mid = parents_mid.reshape(1, CELLS_MID)
    truth = jnp.pad(observations[0], ((0, FIELD_ROWS - FIELDS), (0, 0)))
    truth = jnp.concatenate([truth] * LOCAL, 1)

    tiles = fine_tiles(x0.reshape(LOCAL * CHANNELS, CELLS_IN), neighbours_fine)
    mine, other = gather_weights(weight_first, weight_second, weight_head, x, tiles)
    x2, pred, saved = forward(
        place, mine, other, x0, tiles, parents_fine, neighbours_mid, parents_mid
    )
    pair = jnp.stack([pred, shift(pred, "z_lo", 2, 1)])
    cohort = [pair] + [shift(pair, "x", 4, s) for s in (1, 2, 3)]
    kept, sent = backward(place, cohort, pred, truth, x2, saved, x0, tiles, parents_fine, neighbours_mid, parents_mid)
    grad_first, grad_second, grad_head = reduce_gradients(kept, sent, x)
    return grad_first, grad_second, grad_head.T


def solution(mesh):
    fine_mesh = Mesh(mesh.devices.reshape(2, 4, 4, 4, 2), ("z_lo", "x", "z_hi", "y", "core"))
    placed = (
        P(DP, MEM, None, None),
        P(None, DP, None),
        P(None, DP, None),
        P(None, DP),
        P(),
        P(),
        P(),
        P(),
        P(DP, None, None),
    )
    return jax.shard_map(
        per_device,
        mesh=fine_mesh,
        in_specs=placed,
        out_specs=(P(None, DP, None), P(None, DP, None), P(None, DP)),
        check_vma=False,
    )
```

```python
import math

import jax
import jax.numpy as jnp
from jax import lax
from jax.experimental import pallas as pl
from jax.experimental.pallas import tpu as pltpu
from jax.sharding import Mesh
from jax.sharding import PartitionSpec as P

DP = ("z_hi", "y", "core")
MEM = ("z_lo", "x")

MEMBERS = 16
CHANNELS = 256
SLOTS = 7
FIELDS = 69
FIELD_ROWS = 72
CELLS_OUT = 64
CELLS_MID = 256
CELLS_IN = 1024
SAMPLES = 32
LOCAL = 2
QUARTER = 1024
SMOOTH = 0.0001
NORM = MEMBERS / math.sqrt(SAMPLES * CELLS_OUT)
SECOND_AT = SLOTS * CHANNELS
HEAD_AT = 2 * SLOTS * CHANNELS
PART = 896
SHARE = 32
WIDTH = HEAD_AT + 128
MIB = 1024 * 1024
TILES_MIB = 24
SAVED_ROWS = 8192
MID_AT, SLOPE1_AT, W_AT, SLOPE2_AT = 0, 3584, 5632, 7680

f32 = jnp.float32
bf16 = jnp.bfloat16


def dot(a, b):
    return lax.dot_general(a, b, (((1,), (0,)), ((), ())), preferred_element_type=f32)


def dot_bt(a, b):
    return lax.dot_general(a, b, (((1,), (1,)), ((), ())), preferred_element_type=f32)


def dot_at(a, b):
    return lax.dot_general(a, b, (((0,), (0,)), ((), ())), preferred_element_type=f32)


def one_hot(index_row, rows):
    shape = (rows, index_row.shape[1])
    return jnp.where(lax.broadcasted_iota(jnp.int32, shape, 0) == index_row, 1.0, 0.0).astype(bf16)


def tiles_kernel(x_ref, nb_ref, out_ref):
    row = nb_ref[pl.ds(pl.program_id(0) + 1, 1), :]
    tile = dot(x_ref[...], one_hot(row, CELLS_IN)).astype(bf16)
    for m in range(LOCAL):
        out_ref[m, 0] = tile[m * CHANNELS : (m + 1) * CHANNELS]


def fine_tiles(x0, nb):
    return pl.pallas_call(
        tiles_kernel,
        grid=(SLOTS - 1,),
        in_specs=[
            pl.BlockSpec((LOCAL * CHANNELS, CELLS_IN), lambda j: (0, 0)),
            pl.BlockSpec((SLOTS, CELLS_IN), lambda j: (0, 0)),
        ],
        out_specs=pl.BlockSpec((LOCAL, 1, CHANNELS, CELLS_IN), lambda j: (0, j, 0, 0)),
        out_shape=pltpu.HBM((LOCAL, SLOTS - 1, CHANNELS, CELLS_IN), bf16),
        compiler_params=pltpu.CompilerParams(vmem_limit_bytes=TILES_MIB * MIB),
        cost_estimate=pl.CostEstimate(flops=6_500_000_000, bytes_accessed=8_000_000, transcendentals=0),
        name="fine_tiles",
    )(x0, nb)


def forward_kernel(
    place_ref, mine_ref, other_ref, x_ref, parents_ref, nb_mid_ref, parents_mid_ref, tiles_hbm,
    x2_ref, pred_ref, copies_ref, saved_hbm,
    tiles_ref, w_ref, saved_ref, select_ref, in_sem, out_sem,
):
    loads = [pltpu.make_async_copy(tiles_hbm.at[m], tiles_ref.at[m], in_sem.at[m]) for m in range(LOCAL)]
    for load in loads:
        load.start()
    first, z = place_ref[0] == 0, place_ref[1]
    group = lane_group(16)

    def both_rows(block, lanes):
        mine, other = mine_ref[block, :, lanes].astype(f32), other_ref[block, :, lanes].astype(f32)
        return jnp.concatenate([jnp.where(first, mine, other), jnp.where(first, other, mine)], 0)

    for y in range(4):
        rows = [pl.ds(pl.multiple_of((lax.rem(z - back + 4, 4) * 4 + y) * 16, 16), 16) for back in range(4)]
        for x in range(4):
            for back in range(4):
                part = both_rows(x * 4 + y, slice(back * PART, (back + 1) * PART))
                w_ref[rows[back], x * PART : (x + 1) * PART] = part.astype(bf16)
        shares = [both_rows(x * 4 + y, slice(HEAD_AT, WIDTH)) for x in range(4)]
        for back in range(4):
            head = jnp.zeros((16, 128), f32)
            for x in range(4):
                head = jnp.where(group == x, pltpu.roll(shares[x], (x - back) % 4 * SHARE, 1), head)
            w_ref[rows[back], HEAD_AT:WIDTH] = head.astype(bf16)
    saved_ref[W_AT + SECOND_AT : SLOPE2_AT, 128:256] = jnp.zeros((CHANNELS, 128), bf16)
    saved_ref[W_AT + SECOND_AT : SLOPE2_AT, 0:128] = w_ref[:, HEAD_AT : HEAD_AT + 128]
    for j in range(SLOTS):
        at = SECOND_AT + j * CHANNELS
        saved_ref[W_AT + j * CHANNELS : W_AT + (j + 1) * CHANNELS] = w_ref[:, at : at + CHANNELS]
    stores = []

    def save(begin, end):
        rows = slice(begin, end)
        stores.append(pltpu.make_async_copy(saved_ref.at[rows], saved_hbm.at[rows], out_sem.at[len(stores)]))
        stores[-1].start()

    save(W_AT, SLOPE2_AT)
    unpool = one_hot(parents_ref[...], CELLS_MID)
    for j in range(1, SLOTS):
        select_ref[j - 1] = one_hot(nb_mid_ref[j : j + 1, :], CELLS_MID)
    x1 = []
    for m in range(LOCAL):
        loads[m].wait()
        pooled = jnp.zeros((CHANNELS, CELLS_MID), f32)
        for at in range(0, CELLS_IN, 512):
            cells = slice(at, at + 512)
            a1 = dot(w_ref[:, 0:CHANNELS], x_ref[m, :, cells])
            for j in range(1, SLOTS):
                a1 = a1 + dot(w_ref[:, j * CHANNELS : (j + 1) * CHANNELS], tiles_ref[m, j - 1, :, cells])
            gate = jax.nn.sigmoid(a1)
            slope1 = (gate * (1.0 + a1 * (1.0 - gate))).astype(bf16)
            for half in range(2):
                row = SLOPE1_AT + m * CELLS_IN + at + half * 256
                saved_ref[row : row + 256] = slope1[:, half * 256 : (half + 1) * 256]
            h1 = (x_ref[m, :, cells].astype(f32) + a1 * gate).astype(bf16)
            pooled = pooled + dot_bt(h1, unpool[:, cells])
        save(SLOPE1_AT + m * CELLS_IN, SLOPE1_AT + (m + 1) * CELLS_IN)
        x1.append((pooled * 0.25).astype(bf16))
        saved_ref[m * SECOND_AT : m * SECOND_AT + CHANNELS] = x1[m]
    both = jnp.concatenate(x1, 0)
    for j in range(1, SLOTS):
        tile = dot(both, select_ref[j - 1]).astype(bf16)
        for m in range(LOCAL):
            row = m * SECOND_AT + j * CHANNELS
            saved_ref[row : row + CHANNELS] = tile[m * CHANNELS : (m + 1) * CHANNELS]
    save(MID_AT, SLOPE1_AT)
    pool = one_hot(parents_mid_ref[...], CELLS_OUT)
    for m in range(LOCAL):
        a2 = dot(w_ref[:, SECOND_AT:HEAD_AT], saved_ref[m * SECOND_AT : (m + 1) * SECOND_AT])
        gate2 = jax.nn.sigmoid(a2)
        row = SLOPE2_AT + m * CHANNELS
        saved_ref[row : row + CHANNELS] = (gate2 * (1.0 + a2 * (1.0 - gate2))).astype(bf16)
        h2 = (x1[m].astype(f32) + a2 * gate2).astype(bf16)
        x2_ref[:, m * CELLS_OUT : (m + 1) * CELLS_OUT] = (dot_bt(h2, pool) * 0.25).astype(bf16)
    save(SLOPE2_AT, SAVED_ROWS)
    pred = dot_at(w_ref[:, HEAD_AT : HEAD_AT + 128], x2_ref[...])
    pred_ref[...] = pred[0:FIELD_ROWS]
    for peer in range(MEMBERS // LOCAL):
        copies_ref[peer] = pred[0:FIELD_ROWS]
    for store in stores:
        store.wait()


def lane_group(rows):
    return lax.div(lax.broadcasted_iota(jnp.int32, (rows, 128), 1), SHARE)


def spread_kernel(own_ref, back1_ref, back2_ref, back3_ref, out_ref):
    sources = (own_ref, back1_ref, back2_ref, back3_ref)
    head = own_ref[:, PART:QUARTER].astype(f32)
    for back in range(1, 4):
        head = head + pltpu.roll(sources[back][:, PART:QUARTER].astype(f32), back * SHARE, 1)
    head = head.astype(bf16)
    for block in range(16):
        for back in range(4):
            out_ref[block, :, back * PART : (back + 1) * PART] = sources[back][:, 0:PART]
        out_ref[block, :, HEAD_AT:WIDTH] = head


def spread(pieces):
    return pl.pallas_call(
        spread_kernel,
        in_specs=[pl.BlockSpec(memory_space=pltpu.VMEM)] * 4,
        out_specs=pl.BlockSpec(memory_space=pltpu.VMEM),
        out_shape=jax.ShapeDtypeStruct((16, 8, WIDTH), bf16),
        compiler_params=pltpu.CompilerParams(vmem_limit_bytes=8 * MIB),
        name="spread",
    )(*pieces)


def after_kernel(value_ref, first_ref, out_ref):
    del value_ref, first_ref, out_ref


def after(value, first):
    return pl.pallas_call(
        after_kernel,
        in_specs=[pl.BlockSpec(memory_space=pl.ANY)] * 2,
        out_specs=pl.BlockSpec(memory_space=pl.ANY),
        out_shape=jax.ShapeDtypeStruct(value.shape, value.dtype),
        input_output_aliases={0: 0},
        compiler_params=pltpu.CompilerParams(vmem_limit_bytes=48 * MIB),
        name="after",
    )(value, first)


VMEM = pl.BlockSpec(memory_space=pltpu.VMEM)
HBM = pl.BlockSpec(memory_space=pltpu.HBM)
SMEM = pl.BlockSpec(memory_space=pltpu.SMEM)
TILES = (LOCAL, SLOTS - 1, CHANNELS, CELLS_IN)


def forward(place, mine, other, x0, tiles, parents_fine, nb_mid, parents_mid):
    return pl.pallas_call(
        forward_kernel,
        in_specs=[SMEM, VMEM, VMEM, VMEM, VMEM, VMEM, VMEM, HBM],
        out_specs=[VMEM, VMEM, VMEM, HBM],
        out_shape=[
            jax.ShapeDtypeStruct((CHANNELS, LOCAL * CELLS_OUT), bf16),
            jax.ShapeDtypeStruct((FIELD_ROWS, LOCAL * CELLS_OUT), f32),
            jax.ShapeDtypeStruct((MEMBERS // LOCAL, FIELD_ROWS, LOCAL * CELLS_OUT), f32),
            pltpu.HBM((SAVED_ROWS, CELLS_MID), bf16),
        ],
        scratch_shapes=[
            pltpu.VMEM(TILES, bf16),
            pltpu.VMEM((CHANNELS, WIDTH), bf16),
            pltpu.VMEM((SAVED_ROWS, CELLS_MID), bf16),
            pltpu.VMEM((SLOTS - 1, CELLS_MID, CELLS_MID), bf16),
            pltpu.SemaphoreType.DMA((LOCAL,)),
            pltpu.SemaphoreType.DMA((5,)),
        ],
        compiler_params=pltpu.CompilerParams(vmem_limit_bytes=48 * MIB),
        cost_estimate=pl.CostEstimate(flops=3_200_000_000, bytes_accessed=14_000_000, transcendentals=700_000),
        name="forward",
    )(place, mine, other, x0, parents_fine, nb_mid, parents_mid, tiles)


def sign_smooth(v):
    return v * lax.rsqrt(v * v + SMOOTH)


def backward_kernel(
    place_ref, cohort_ref, own_ref, obs_ref, x2_ref,
    parents_ref, nb_mid_ref, parents_mid_ref, saved_hbm, x_hbm, tiles_hbm,
    kept_ref, sent_ref,
    saved_ref, x_ref, tiles_ref, g1_ref, select_ref, unpool_ref, sem,
):
    early, late = pl.ds(W_AT, SAVED_ROWS - W_AT), pl.ds(0, W_AT)
    moves = (
        (saved_hbm.at[early], saved_ref.at[early]), (saved_hbm.at[late], saved_ref.at[late]), (x_hbm, x_ref), (tiles_hbm, tiles_ref)
    )
    loads = [pltpu.make_async_copy(source, here, sem.at[i]) for i, (source, here) in enumerate(moves)]
    for load in loads:
        load.start()
    first = place_ref[0] == 0

    def put_rows(quarter, y, lanes, value0, value1):
        kept_ref[quarter, y, :, lanes] = jnp.where(first, value0, value1).astype(bf16)
        sent_ref[quarter, y, :, lanes] = jnp.where(first, value1, value0).astype(bf16)

    def put(piece, value):
        at = piece * 256
        cuts = [0, 128, 256] if at // PART != (at + 128) // PART else [0, 256]
        for begin, end in zip(cuts[:-1], cuts[1:]):
            quarter, offset = (at + begin) // PART, (at + begin) % PART
            for z in range(4):
                lanes = slice(z * PART + offset, z * PART + offset + end - begin)
                for y in range(4):
                    row = (z * 4 + y) * 16
                    put_rows(quarter, y, lanes, value[row : row + 8, begin:end], value[row + 8 : row + 16, begin:end])

    def put_head(value):
        group = lane_group(16)
        for quarter in range(4):
            for y in range(4):
                packed = jnp.zeros((16, 128), f32)
                for z in range(4):
                    row = (z * 4 + y) * 16
                    packed = jnp.where(group == z, pltpu.roll(value[row : row + 16], (z - quarter) % 4 * SHARE, 1), packed)
                put_rows(quarter, y, slice(HEAD_AT, WIDTH), packed[0:8], packed[8:16])

    own = own_ref[...]
    spread = jnp.zeros_like(own)
    for peer in range(MEMBERS // LOCAL):
        theirs = cohort_ref[peer]
        spread = spread + sign_smooth(own - theirs) + sign_smooth(own - pltpu.roll(theirs, CELLS_OUT, 1))
    skill = sign_smooth(own - obs_ref[...])
    slope = NORM * (skill / MEMBERS - spread / (MEMBERS * (MEMBERS - 1)))
    slope = jnp.concatenate([slope, jnp.zeros((128 - FIELD_ROWS, 128), f32)], 0).astype(bf16)
    put_head(dot_bt(x2_ref[...], slope))
    pool = one_hot(parents_mid_ref[...], CELLS_OUT)
    wide = [dot(slope[:, m * CELLS_OUT : (m + 1) * CELLS_OUT], pool).astype(bf16) for m in range(LOCAL)]
    for j in range(1, SLOTS):
        select_ref[j - 1] = one_hot(nb_mid_ref[j : j + 1, :], CELLS_MID)
    unpool_ref[...] = one_hot(parents_ref[...], CELLS_MID)
    loads[0].wait()
    head_t = saved_ref[W_AT + SECOND_AT : SLOPE2_AT, 0:128]
    dh2 = [dot(head_t, wide[m]) * 0.25 for m in range(LOCAL)]
    slope2 = saved_ref[SLOPE2_AT:SAVED_ROWS].astype(f32)
    g2 = [(dh2[m] * slope2[m * CHANNELS : (m + 1) * CHANNELS]).astype(bf16) for m in range(LOCAL)]
    both = jnp.concatenate(g2, 0)
    back = [dh2[m] + dot_at(saved_ref[W_AT : W_AT + CHANNELS], g2[m]) for m in range(LOCAL)]
    for q in range(1, SLOTS):
        spread_back = dot_bt(both, select_ref[q - 1]).astype(bf16)
        weight = saved_ref[W_AT + q * CHANNELS : W_AT + (q + 1) * CHANNELS]
        for m in range(LOCAL):
            back[m] = back[m] + dot_at(weight, spread_back[m * CHANNELS : (m + 1) * CHANNELS])
    loads[1].wait()
    for m in range(LOCAL):
        dh1 = dot((back[m] * 0.25).astype(bf16), unpool_ref[...])
        for at in range(0, CELLS_IN, 256):
            slope1 = saved_ref[SLOPE1_AT + m * CELLS_IN + at : SLOPE1_AT + m * CELLS_IN + at + 256].astype(f32)
            g1_ref[m, :, at : at + 256] = (dh1[:, at : at + 256] * slope1).astype(bf16)
    for load in loads[2:]:
        load.wait()
    for q in range(SLOTS):
        row0, row1 = q * CHANNELS, SECOND_AT + q * CHANNELS
        grad = dot_bt(g2[0], saved_ref[row0 : row0 + CHANNELS]) + dot_bt(g2[1], saved_ref[row1 : row1 + CHANNELS])
        put(SLOTS + q, grad)
    put(0, dot_bt(g1_ref[0], x_ref[0]) + dot_bt(g1_ref[1], x_ref[1]))
    for j in range(1, SLOTS):
        grad = dot_bt(g1_ref[0], tiles_ref[0, j - 1]) + dot_bt(g1_ref[1], tiles_ref[1, j - 1])
        put(j, grad)


def backward(place, cohort, own, obs, x2, saved, x0, tiles, parents_fine, nb_mid, parents_mid):
    return pl.pallas_call(
        backward_kernel,
        in_specs=[SMEM] + [VMEM] * 7 + [HBM] * 3,
        out_specs=[VMEM] * 2,
        out_shape=[jax.ShapeDtypeStruct((4, 4, 8, WIDTH), bf16)] * 2,
        scratch_shapes=[
            pltpu.VMEM((SAVED_ROWS, CELLS_MID), bf16),
            pltpu.VMEM((LOCAL, CHANNELS, CELLS_IN), bf16),
            pltpu.VMEM(TILES, bf16),
            pltpu.VMEM((LOCAL, CHANNELS, CELLS_IN), bf16),
            pltpu.VMEM((SLOTS - 1, CELLS_MID, CELLS_MID), bf16),
            pltpu.VMEM((CELLS_MID, CELLS_IN), bf16),
            pltpu.SemaphoreType.DMA((4,)),
        ],
        compiler_params=pltpu.CompilerParams(vmem_limit_bytes=50 * MIB),
        cost_estimate=pl.CostEstimate(flops=4_000_000_000, bytes_accessed=16_000_000, transcendentals=200_000),
        name="backward",
    )(place, cohort, own, obs, x2, parents_fine, nb_mid, parents_mid, saved, x0, tiles)


def shift(v, axis, n, by):
    return lax.ppermute(v, axis, [(i, (i + by) % n) for i in range(n)])


def gather_weights(weight_first, weight_second, weight_head, x, tiles):
    rows = weight_first.shape[1]
    flat = jnp.concatenate(
        [
            weight_first.transpose(1, 0, 2).reshape(rows, SECOND_AT),
            weight_second.transpose(1, 0, 2).reshape(rows, SECOND_AT),
            weight_head.T,
            jnp.zeros((rows, WIDTH - HEAD_AT - FIELDS), bf16),
        ],
        1,
    )
    mine = jnp.concatenate(
        [
            lax.dynamic_slice_in_dim(flat, x * PART, PART, 1),
            lax.dynamic_slice_in_dim(flat, HEAD_AT + x * SHARE, SHARE, 1),
            jnp.zeros((rows, QUARTER - PART - SHARE), bf16),
        ],
        1,
    )
    column = spread([mine] + [shift(mine, "z_hi", 4, s) for s in (1, 2, 3)])
    plane = after(lax.all_to_all(column, ("x", "y"), 0, 0), tiles)
    return plane, shift(plane, "core", 2, 1)


def fold_kernel(plane_ref, out_ref):
    total = plane_ref[0].astype(f32)
    for block in range(1, 16):
        total = total + plane_ref[block].astype(f32)
    head, group = total[:, HEAD_AT:WIDTH], lane_group(8)
    for z in range(4):
        share = jnp.where(group == 0, pltpu.roll(head, -z % 4 * SHARE, 1), 0.0).astype(bf16)
        for low in range(2):
            out_ref[z * 2 + low, :, 0:PART] = total[:, z * PART : (z + 1) * PART].astype(bf16)
            out_ref[z * 2 + low, :, PART:QUARTER] = share


def fold(plane):
    return pl.pallas_call(
        fold_kernel,
        in_specs=[VMEM],
        out_specs=VMEM,
        out_shape=jax.ShapeDtypeStruct((8, 8, QUARTER), bf16),
        compiler_params=pltpu.CompilerParams(vmem_limit_bytes=8 * MIB),
        name="fold",
    )(plane)


def reduce_gradients(kept, sent, x):
    total = (kept.astype(f32) + shift(sent, "core", 2, 1).astype(f32)).astype(bf16)
    column = fold(lax.all_to_all(total.reshape(16, 8, WIDTH), ("x", "y"), 0, 0))
    column = lax.all_to_all(column, ("z_hi", "z_lo"), 0, 0)
    total = jnp.sum(column.astype(f32), 0).astype(bf16)
    return finish(x.astype(jnp.int32).reshape(1), [total] + [shift(total, "x", 4, s) for s in (1, 2, 3)])


def finish_kernel(x_ref, own_ref, back1_ref, back2_ref, back3_ref, first_ref, second_ref, head_ref, flat_ref, heads_ref):
    for back, source in enumerate((own_ref, back1_ref, back2_ref, back3_ref)):
        quarter = lax.rem(x_ref[0] - back + 4, 4)
        flat_ref[:, pl.ds(pl.multiple_of(quarter * PART, 128), PART)] = source[:, 0:PART].astype(f32)
        heads_ref[quarter] = source[:, PART:QUARTER].astype(f32)
    for j in range(SLOTS):
        first_ref[j] = flat_ref[:, j * CHANNELS : (j + 1) * CHANNELS]
        second_ref[j] = flat_ref[:, SECOND_AT + j * CHANNELS : SECOND_AT + (j + 1) * CHANNELS]
    head = heads_ref[0]
    for x in range(1, 4):
        head = head + pltpu.roll(heads_ref[x], x * SHARE, 1)
    head_ref[...] = head[:, 0:FIELDS]


def finish(x, quarters):
    return pl.pallas_call(
        finish_kernel,
        in_specs=[SMEM] + [VMEM] * 4,
        out_specs=[VMEM] * 3,
        out_shape=[
            jax.ShapeDtypeStruct((SLOTS, 8, CHANNELS), f32),
            jax.ShapeDtypeStruct((SLOTS, 8, CHANNELS), f32),
            jax.ShapeDtypeStruct((8, FIELDS), f32),
        ],
        scratch_shapes=[pltpu.VMEM((8, HEAD_AT), f32), pltpu.VMEM((4, 8, 128), f32)],
        compiler_params=pltpu.CompilerParams(vmem_limit_bytes=16 * MIB),
        name="finish",
    )(x, *quarters)


def per_device(
    member_fields, weight_first, weight_second, weight_head,
    neighbours_fine, neighbours_mid, parents_fine, parents_mid, observations,
):
    core, x = lax.axis_index("core"), lax.axis_index("x")
    place = jnp.stack([core, lax.axis_index("z_hi")]).astype(jnp.int32)
    x0 = member_fields[0]
    parents_fine = parents_fine.reshape(1, CELLS_IN)
    parents_mid = parents_mid.reshape(1, CELLS_MID)
    truth = jnp.pad(observations[0], ((0, FIELD_ROWS - FIELDS), (0, 0)))
    truth = jnp.concatenate([truth] * LOCAL, 1)

    tiles = fine_tiles(x0.reshape(LOCAL * CHANNELS, CELLS_IN), neighbours_fine)
    mine, other = gather_weights(weight_first, weight_second, weight_head, x, tiles)
    x2, pred, copies, saved = forward(
        place, mine, other, x0, tiles, parents_fine, neighbours_mid, parents_mid
    )
    cohort = lax.all_to_all(copies, MEM, 0, 0)
    kept, sent = backward(place, cohort, pred, truth, x2, saved, x0, tiles, parents_fine, neighbours_mid, parents_mid)
    grad_first, grad_second, grad_head = reduce_gradients(kept, sent, x)
    return grad_first, grad_second, grad_head.T


def solution(mesh):
    fine_mesh = Mesh(mesh.devices.reshape(2, 4, 4, 4, 2), ("z_lo", "x", "z_hi", "y", "core"))
    placed = (
        P(DP, MEM, None, None),
        P(None, DP, None),
        P(None, DP, None),
        P(None, DP),
        P(),
        P(),
        P(),
        P(),
        P(DP, None, None),
    )
    return jax.shard_map(
        per_device,
        mesh=fine_mesh,
        in_specs=placed,
        out_specs=(P(None, DP, None), P(None, DP, None), P(None, DP)),
        check_vma=False,
    )
```
